32 devices in a mesh: front: 4 (over y, x), row: 2 (over core), col: 4 (over z).
Axes of the slice: x: 2, y: 2, z: 4, core: 2. Of those that a mesh axis runs over, the one named last changes fastest.
Arguments:
- front: bfloat16 [4, 12288, 12288], P('front', 'row', 'col'), may hold values from -6 to 6
- panel: bfloat16 [4, 12288, 512], P('front', ('row', 'col')), may hold values from -8 to 8
- inverse: bfloat16 [4, 512, 512], P('front'), may hold values from -0.0046 to 0.056
- fill: int32 [4, 48], P('front'), may hold values 0 or 1
- block_map: int32 [4, 48], P('front'), may hold values from 0 to 47, as said below
- parent_front: bfloat16 [4, 6144, 12288], P('front', 'row', 'col'), may hold values from -6 to 6
Outputs:
- factor_rows: bfloat16 [4, 12288, 512], P('front', ('row', 'col'))
- parent: float32 [4, 6144, 12288], P('front', 'row', 'col')
The draws below stay inside these ranges and needn't reach their ends.
Inputs may be any that keep to these rules, and one draw needn't show every extreme that they name: `block_map`: each front's map is a permutation of its blocks that keeps every aligned group of 12 blocks in place as a group.
All inputs are finite; a program needn't handle non-finite values. No bound on the sum of `fill` on one device may be relied on, other than what follows from the above.
Results may differ from the reference program's by a relative error of at most 0.0025.
Values may be sent and summed in bfloat16 or wider, within the bound.
No kernel may reach another device: no remote copies, remote signals or barrier semaphores. Data moves between devices by JAX's collectives and lax.ppermute only.
A program may use at most 320 MiB of HBM per device.

```python
import jax
import jax.numpy as jnp

M = 12288
PIVOTS = 512
BLK = 256
NF = 4
NBLK = 48
GRP = 12
TILE = 6144
HALF = 6144
N_ROW = 2


def draw_block_map(key, part):
    group_total = NBLK // GRP

    def one_front(front_key):
        group_keys = jax.random.split(front_key, group_total)
        orders = jax.vmap(lambda member_key: jax.random.permutation(member_key, GRP))(group_keys)
        shifted = orders + (jnp.arange(group_total, dtype=jnp.int32) * GRP)[:, None]
        return shifted.reshape(NBLK).astype(jnp.int32)
    return jax.vmap(one_front)(jax.random.split(key, NF))


def draw_inverse(key, part):
    diag_key, spread_key = jax.random.split(jax.random.fold_in(key, 7))
    diagonal = jax.random.uniform(diag_key, (NF, PIVOTS), jnp.float32, 0.035, 0.055)
    spread = jnp.clip(0.0013 * jax.random.normal(spread_key, (NF, PIVOTS, PIVOTS), jnp.float32), -0.0045, 0.0045)
    identity = jnp.eye(PIVOTS, dtype=jnp.float32)
    whole = spread * (1.0 - identity)[None] + diagonal[:, :, None] * identity[None]
    return whole.astype(jnp.bfloat16)


def touch_ends(drawn, rng, smallest, high):
    longest = drawn.shape.index(max(drawn.shape))
    spots = []
    for shift in (0, 1):
        where = [jax.random.randint(jax.random.fold_in(rng, axis), (), 0, length) for axis, length in enumerate(drawn.shape)]
        where[longest] = (where[longest] + shift) % drawn.shape[longest]
        spots.append(tuple(where))
    return drawn.at[spots[0]].set(smallest).at[spots[1]].set(high)


def level_of(key, dims, pieces, low, largest):
    def one(axis_at, shards_of):
        steps = jax.random.uniform(jax.random.fold_in(jax.random.fold_in(key, 6), axis_at), (shards_of,), jnp.float32, low / len(pieces), largest / len(pieces))
        return jnp.repeat(jnp.exp(steps), dims[axis_at] // shards_of).reshape((-1,) + (1,) * (len(dims) - axis_at - 1))

    loudness = one(*pieces[0])
    for cut in pieces[1:]:
        loudness = loudness * one(*cut)
    return loudness


def scatter_about(own_key, shape, scale, reach, pieces=(), kind=jnp.bfloat16):
    array = scale * jax.random.normal(own_key, shape, jnp.float32)
    if pieces:
        array = array * level_of(own_key, shape, pieces, -0.22, 0.18)
    return jnp.clip(array, -reach, reach).astype(kind)


def setup_inputs(seed: int = 0) -> dict:
    key_list = jax.random.split(jax.random.key(seed), 7)
    return {
        "front": scatter_about(key_list[0], (NF, M, M), 1.0, 6.0, ((0, 4), (1, 2), (2, 4))),
        "panel": scatter_about(key_list[1], (NF, M, PIVOTS), 2.5, 8.0, ((0, 4), (1, 8))),
        "inverse": draw_inverse(jax.random.fold_in(key_list[6], 71), 0),
        "fill": touch_ends((jax.random.randint(key_list[3], (NF, NBLK), 0, 3) < 2).astype(jnp.int32), jax.random.fold_in(key_list[3], 1), 0, 1),
        "block_map": draw_block_map(jax.random.fold_in(key_list[6], 71), 0),
        "parent_front": scatter_about(key_list[5], (NF, HALF, M), 1.0, 6.0, ((0, 4), (1, 2), (2, 4))),
    }


def block_inverse(mapping, block_total):
    target = jnp.arange(block_total, dtype=jnp.int32)
    matches = (mapping[:, None] == target[None, :]).astype(jnp.int32)
    return jnp.sum(matches * target[:, None], axis=0).astype(jnp.int32)


def reference(front, panel, inverse, fill, block_map, parent_front):
    factors = []
    contributions = []
    for member in range(NF):
        row_fill = jnp.repeat(fill[member], BLK).astype(jnp.bfloat16)
        masked = panel[member] * row_fill[:, None]
        factor = jnp.dot(masked, jnp.triu(inverse[member]), preferred_element_type=jnp.float32).astype(jnp.bfloat16)
        factors.append(factor)
        schur = front[member].astype(jnp.float32) - jnp.dot(factor, factor.T, preferred_element_type=jnp.float32)
        source = block_inverse(block_map[member], NBLK)
        blocked = jnp.take(schur.reshape(NBLK, BLK, NBLK, BLK), source, axis=0)
        blocked = jnp.take(blocked, source, axis=2)
        contributions.append(blocked.reshape(M, M).astype(jnp.bfloat16))
    halves = []
    for member in range(NF):
        paired = member // 2 * 2
        summed = contributions[paired].astype(jnp.float32) + contributions[paired + 1].astype(jnp.float32)
        layout = summed.reshape(N_ROW, 2, TILE // 2, M)[:, member % 2].reshape(HALF, M)
        halves.append(parent_front[member].astype(jnp.float32) + layout)
    return jnp.stack(factors), jnp.stack(halves)
```

```python
import functools

import jax
import jax.numpy as jnp
from jax import lax
from jax.experimental import pallas as pl
from jax.experimental.pallas import tpu as pltpu
from jax.sharding import PartitionSpec as P

BLK = 256
NT = (((1,), (1,)), ((), ()))
VMEM_LIMIT = 48 * 1024 * 1024


def block_inverse(mapping):
    block_total = mapping.shape[0]
    target = jnp.arange(block_total, dtype=jnp.int32)
    matches = (mapping[:, None] == target[None, :]).astype(jnp.int32)
    return jnp.sum(matches * target[:, None], axis=0)


def cost(flops, moved):
    return pl.CostEstimate(flops=int(flops), bytes_accessed=int(moved), transcendentals=0)


def update_kernel(unit, stride, offset, rows_ref, fac_ref, front_ref, factor_ref, col_ref, out_ref):
    first = (pl.program_id(1) * stride + offset) * unit
    col = col_ref[pl.ds(pl.multiple_of(first, unit), unit), :]
    product = lax.dot_general(factor_ref[...], col, NT, preferred_element_type=jnp.float32)
    out_ref[...] = (front_ref[...].astype(jnp.float32) - product).astype(jnp.bfloat16)


def updated_blocks(front, rows, factor, factor_rows, col_side, unit, stride, offset, units):
    count = rows.shape[0]
    pivots = factor.shape[1]
    grid_spec = pltpu.PrefetchScalarGridSpec(
        num_scalar_prefetch=2,
        grid=(count, units),
        in_specs=[
            pl.BlockSpec((BLK, unit), lambda i, j, rows, fac: (rows[i], j * stride + offset)),
            pl.BlockSpec((BLK, pivots), lambda i, j, rows, fac: (fac[i], 0)),
            pl.BlockSpec(col_side.shape, lambda i, j, rows, fac: (0, 0)),
        ],
        out_specs=pl.BlockSpec((BLK, unit), lambda i, j, rows, fac: (i, j)),
    )
    return pl.pallas_call(
        functools.partial(update_kernel, unit, stride, offset),
        grid_spec=grid_spec,
        out_shape=jax.ShapeDtypeStruct((count * BLK, units * unit), jnp.bfloat16),
        compiler_params=pltpu.CompilerParams(vmem_limit_bytes=VMEM_LIMIT),
        cost_estimate=cost(
            2 * count * BLK * units * unit * pivots, 4 * count * BLK * units * unit + 2 * col_side.size
        ),
    )(rows, factor_rows, front, factor, col_side)


def pick_kernel(rows_ref, front_ref, out_ref):
    out_ref[...] = front_ref[...]


def picked_blocks(front, rows, unit, stride, offset, units):
    count = rows.shape[0]
    grid_spec = pltpu.PrefetchScalarGridSpec(
        num_scalar_prefetch=1,
        grid=(count, units),
        in_specs=[pl.BlockSpec((BLK, unit), lambda i, j, rows: (rows[i], j * stride + offset))],
        out_specs=pl.BlockSpec((BLK, unit), lambda i, j, rows: (i, j)),
    )
    return pl.pallas_call(
        pick_kernel,
        grid_spec=grid_spec,
        out_shape=jax.ShapeDtypeStruct((count * BLK, units * unit), jnp.bfloat16),
        compiler_params=pltpu.CompilerParams(vmem_limit_bytes=VMEM_LIMIT),
        cost_estimate=cost(0, 4 * count * BLK * units * unit),
    )(rows, front)


def add_kernel(
    blocks, pieces, target_ref, own_ref, place_ref, front_ref, factor_ref, col_ref, given_ref, *refs
):
    piece_refs, out_ref = refs[:pieces], refs[-1]
    factor = factor_ref[...]
    for block in range(blocks):
        here = pl.ds(block * BLK, BLK)
        own = pl.ds(pl.multiple_of(place_ref[0, block] * BLK, BLK), BLK)
        product = lax.dot_general(factor, col_ref[own, :], NT, preferred_element_type=jnp.float32)
        kept = (front_ref[:, own].astype(jnp.float32) - product).astype(jnp.bfloat16)
        arrived = piece_refs[0][:, pl.ds(pl.multiple_of(place_ref[1, block] * BLK, BLK), BLK)]
        if pieces == 2:
            other = piece_refs[1][:, pl.ds(pl.multiple_of(place_ref[2, block] * BLK, BLK), BLK)]
            arrived = jnp.where(place_ref[3, block] == 0, arrived, other)
        out_ref[:, here] = (
            given_ref[:, here].astype(jnp.float32)
            + kept.astype(jnp.float32)
            + arrived.astype(jnp.float32)
        )


def add_rows(out, targets, owns, places, front, factor, col_side, given, pieces):
    count = targets.shape[0]
    cols = front.shape[1]
    pivots = factor.shape[1]
    blocks = cols // BLK
    in_specs = [
        pl.BlockSpec((BLK, cols), lambda i, targets, owns, places: (owns[i], 0)),
        pl.BlockSpec((BLK, pivots), lambda i, targets, owns, places: (owns[i], 0)),
        pl.BlockSpec(col_side.shape, lambda i, targets, owns, places: (0, 0)),
        pl.BlockSpec((BLK, cols), lambda i, targets, owns, places: (targets[i], 0)),
    ] + [
        pl.BlockSpec((BLK, piece.shape[1]), lambda i, targets, owns, places: (i, 0))
        for piece in pieces
    ]
    operands = [targets, owns, places, front, factor, col_side, given, *pieces]
    aliases = {}
    if out is not None:
        aliases = {len(operands): 0}
        operands.append(out)
        in_specs.append(pl.BlockSpec(memory_space=pl.ANY))
    return pl.pallas_call(
        functools.partial(add_kernel, blocks, len(pieces)),
        grid_spec=pltpu.PrefetchScalarGridSpec(
            num_scalar_prefetch=3,
            grid=(count,),
            in_specs=in_specs,
            out_specs=pl.BlockSpec((BLK, cols), lambda i, targets, owns, places: (targets[i], 0)),
        ),
        out_shape=jax.ShapeDtypeStruct(given.shape, jnp.float32),
        input_output_aliases=aliases,
        compiler_params=pltpu.CompilerParams(vmem_limit_bytes=VMEM_LIMIT),
        cost_estimate=cost(2 * count * BLK * cols * pivots, 10 * count * BLK * cols + 2 * col_side.size),
    )(*operands)


def take_block(table, first, count):
    return lax.dynamic_slice_in_dim(table, first, count, 0)


def line_gather(mine, place, between):
    up = [(0, 1), (1, 2), (2, 3)]
    down = [(1, 0), (2, 1), (3, 2)]
    below = lax.ppermute(mine, "col", up)
    above = lax.ppermute(mine, "col", down)
    below2 = lax.ppermute(below, "col", up[1:])
    above2 = lax.ppermute(above, "col", down[:2])
    far = lax.ppermute(jnp.where(place == 2, below2, above2), "col", [(2, 3), (1, 0)])

    def choose(*options):
        picked = options[-1]
        for index in range(len(options) - 2, -1, -1):
            picked = jnp.where(place == index, options[index], picked)
        return picked

    segments = [
        choose(mine, below, below2, far),
        choose(above, mine, below, below2),
        choose(above2, above, mine, below),
        choose(far, above2, above, mine),
    ]
    low = choose(mine, above, below2, below)
    high = choose(above, above2, below, mine)
    return segments, low, high


def col_rows(low, high, place, core):
    both = jnp.concatenate([low, high], axis=0)
    swapped = lax.ppermute(both, "row", [(0, 1), (1, 0)])
    return jnp.where(core == place // 2, both, swapped)


def factor_of(panel, inverse, fill, first_row):
    local_rows = panel.shape[0]
    positions = (first_row + jnp.arange(local_rows, dtype=jnp.int32)) // BLK
    blocks = jnp.arange(fill.shape[0], dtype=jnp.int32)
    row_fill = jnp.sum(
        (positions[:, None] == blocks[None, :]).astype(jnp.int32) * fill[None, :], axis=1
    )
    masked = panel * row_fill[:, None].astype(jnp.bfloat16)
    return jnp.dot(masked, jnp.triu(inverse), preferred_element_type=jnp.float32).astype(jnp.bfloat16)


def from_sibling(block):
    route = []
    for low in range(0, lax.axis_size("front"), 2):
        route += [(low, low + 1), (low + 1, low)]
    return lax.ppermute(block, "front", route)


def shards(front, panel, inverse, fill, block_map, parent_front):
    front, panel, given = front[0], panel[0], parent_front[0]
    col_count = lax.axis_size("col")
    row_count = lax.axis_size("row")
    core = lax.axis_index("row")
    place = lax.axis_index("col")
    parity = lax.axis_index("front") % 2
    local_rows = panel.shape[0]
    tile_rows, tile_cols = front.shape
    half_blocks = tile_rows // 2 // BLK
    col_blocks = tile_cols // BLK
    seg = local_rows // BLK
    row_base = core * (tile_rows // BLK)
    sibling_map = from_sibling(block_map[0])
    source = block_inverse(block_map[0])
    sibling_source = block_inverse(sibling_map)
    col_source = take_block(source, place * col_blocks, col_blocks) - place * col_blocks
    sibling_cols = take_block(sibling_source, place * col_blocks, col_blocks) - place * col_blocks
    first_row = (core * col_count + place) * local_rows

    closed = half_blocks % col_blocks == 0
    line = (
        row_count == 2 and col_count == 4 and closed and tile_rows == 2 * tile_cols
        and local_rows % (2 * BLK) == 0 and 2 * local_rows == tile_cols
    )
    if not line:
        factor = factor_of(panel, inverse[0], fill[0], first_row)
        all_rows = lax.all_gather(factor, ("row", "col"), axis=0, tiled=True)
        row_side = take_block(all_rows, core * tile_rows, tile_rows)
        col_side = take_block(all_rows, place * tile_cols, tile_cols)
        sent = take_block(source, row_base + (1 - parity) * half_blocks, half_blocks) - row_base
        owns = take_block(source, row_base + parity * half_blocks, half_blocks) - row_base
        targets = jnp.arange(half_blocks, dtype=jnp.int32)
        arrived = from_sibling(
            updated_blocks(front, sent, row_side, sent, col_side, tile_cols, 1, 0, 1)
        )
        places = jnp.stack([col_source, sibling_cols])
        out = add_rows(None, targets, owns, places, front, row_side, col_side, given, [arrived])
        return factor[None], out[None]

    cut = seg // 2
    unit = cut * BLK
    steps = jnp.arange(cut, dtype=jnp.int32)
    sent_half = 1 - parity
    inner = parity * seg
    outer = seg - inner
    starts = [inner, inner + cut, outer, outer + cut]
    sent_base = sent_half * half_blocks
    raw = []
    for start in (starts[0], starts[2]):
        raw.append(from_sibling(picked_blocks(front, sent_base + start + steps, unit, 2, 0, 2)))
    factor = factor_of(panel, inverse[0], fill[0], first_row)
    segments, low, high = line_gather(factor, place, None)
    sibling_part = from_sibling(factor[:unit])
    col_side = col_rows(low, high, place, core)
    inner_rows = jnp.where(parity == 1, segments[1], segments[2])
    outer_rows = jnp.where(parity == 1, segments[0], segments[3])
    arrived = []
    for kind, (start, rows) in enumerate(zip(starts, (inner_rows, inner_rows, outer_rows, outer_rows))):
        fronts = sent_base + start + steps
        if kind % 2 == 0:
            piece = updated_blocks(front, fronts, rows, steps, col_side, unit, 2, 1, 2)
            arrived.append(from_sibling(piece))
        elif kind == 1:
            piece = updated_blocks(front, fronts, rows, steps + cut, col_side, unit, 1, 0, 4)
            arrived.append(from_sibling(piece))
        else:
            arrived.append([
                from_sibling(
                    updated_blocks(front, fronts[i:i + 1], rows, steps[i:i + 1] + cut, col_side, unit, 1, 0, 4)
                )
                for i in range(cut)
            ])

    row_side = jnp.concatenate(segments, axis=0)
    parts, part_low, part_high = line_gather(sibling_part, place, None)
    sibling_col = col_rows(part_low, part_high, place, core)
    kept_inner = jnp.where(parity == 0, parts[1], parts[2])
    kept_outer = jnp.where(parity == 0, parts[0], parts[3])
    finished = [
        updated_blocks(piece, steps, rows, steps, sibling_col, unit, 1, 0, 2)
        for piece, rows in zip(raw, (kept_inner, kept_outer))
    ]
    in_x = sibling_cols % seg < cut
    seg_at = sibling_cols // seg * cut
    places_x = jnp.stack([
        col_source,
        seg_at + jnp.minimum(sibling_cols % seg, cut - 1),
        seg_at + jnp.maximum(sibling_cols % seg - cut, 0),
        jnp.where(in_x, 0, 1),
    ])
    places_y = jnp.stack([col_source, sibling_cols])
    kept_base = row_base + parity * half_blocks
    kept_inner_at = (1 - parity) * seg
    kept_starts = [kept_inner_at, kept_inner_at + cut, seg - kept_inner_at, seg - kept_inner_at + cut]
    out = None
    for kind, start in enumerate(kept_starts):
        landed = take_block(sibling_map, kept_base + start, cut)
        owns = jnp.sum(
            jnp.where(landed[:, None] == jnp.arange(source.shape[0])[None, :], source[None, :], 0), axis=1
        ) - row_base
        targets = landed - kept_base
        if kind % 2 == 0:
            pieces = [finished[kind // 2], arrived[kind]]
            out = add_rows(out, targets, owns, places_x, front, row_side, col_side, given, pieces)
        elif kind == 1:
            out = add_rows(out, targets, owns, places_y, front, row_side, col_side, given, [arrived[kind]])
        else:
            for i in range(cut):
                out = add_rows(
                    out, targets[i:i + 1], owns[i:i + 1], places_y, front, row_side, col_side, given,
                    [arrived[kind][i]],
                )
    return factor[None], out[None]


def solution(mesh):
    placed = (
        P("front", "row", "col"),
        P("front", ("row", "col"), None),
        P("front", None, None),
        P("front", None),
        P("front", None),
        P("front", "row", "col"),
    )
    return jax.shard_map(
        shards,
        mesh=mesh,
        in_specs=placed,
        out_specs=(P("front", ("row", "col"), None), P("front", "row", "col")),
        check_vma=False,
    )
```

```python
import functools

import jax
import jax.numpy as jnp
from jax import lax
from jax.experimental import pallas as pl
from jax.experimental.pallas import tpu as pltpu
from jax.sharding import PartitionSpec as P

BLK = 256
NT = (((1,), (1,)), ((), ()))
VMEM_LIMIT = 48 * 1024 * 1024
STEP = 128
RAW_PIECES = ((0, 1), (1, 4), (5, 5), (10, 2))


def block_inverse(mapping):
    block_total = mapping.shape[0]
    target = jnp.arange(block_total, dtype=jnp.int32)
    matches = (mapping[:, None] == target[None, :]).astype(jnp.int32)
    return jnp.sum(matches * target[:, None], axis=0)


SMALL = pl.CostEstimate(flops=1, bytes_accessed=1, transcendentals=0)


def update_kernel(unit, stride, offset, at_ref, front_ref, factor_ref, col_ref, out_ref):
    first = (pl.program_id(1) * stride + offset) * unit
    col = col_ref[pl.ds(pl.multiple_of(first, unit), unit), :]
    product = lax.dot_general(factor_ref[...], col, NT, preferred_element_type=jnp.float32)
    out_ref[...] = (front_ref[...].astype(jnp.float32) - product).astype(jnp.bfloat16)


def updated_rows(front, at, front_row, factor, factor_row, col_side, grid, height, unit, stride, offset):
    pivots = factor.shape[1]
    return pl.pallas_call(
        functools.partial(update_kernel, unit, stride, offset),
        grid_spec=pltpu.PrefetchScalarGridSpec(
            num_scalar_prefetch=1,
            grid=grid,
            in_specs=[
                pl.BlockSpec((height, unit), lambda i, j, at: (front_row(i, at), j * stride + offset)),
                pl.BlockSpec((height, pivots), lambda i, j, at: (factor_row(i, at), 0)),
                pl.BlockSpec(col_side.shape, lambda i, j, at: (0, 0)),
            ],
            out_specs=pl.BlockSpec((height, unit), lambda i, j, at: (i, j)),
        ),
        out_shape=jax.ShapeDtypeStruct((grid[0] * height, grid[1] * unit), jnp.bfloat16),
        compiler_params=pltpu.CompilerParams(vmem_limit_bytes=VMEM_LIMIT),
        cost_estimate=SMALL,
    )(at, front, factor, col_side)


def pick_kernel(at_ref, front_ref, out_ref):
    out_ref[...] = front_ref[...]


def picked_rows(front, at, front_row, grid, height, unit, stride):
    return pl.pallas_call(
        pick_kernel,
        grid_spec=pltpu.PrefetchScalarGridSpec(
            num_scalar_prefetch=1,
            grid=grid,
            in_specs=[pl.BlockSpec((height, unit), lambda i, j, at: (front_row(i, at), j * stride))],
            out_specs=pl.BlockSpec((height, unit), lambda i, j, at: (i, j)),
        ),
        out_shape=jax.ShapeDtypeStruct((grid[0] * height, grid[1] * unit), jnp.bfloat16),
        compiler_params=pltpu.CompilerParams(vmem_limit_bytes=VMEM_LIMIT),
        cost_estimate=SMALL,
    )(at, front)


def assemble_kernel(plan, sources, at_ref, *refs):
    outs, sem = refs[sources:-1], refs[-1]
    for step, (out, first, rows, choice, options) in enumerate(plan):
        chosen = choice(at_ref)
        for value, (source, start) in options.items():
            @pl.when(chosen == value)
            def _():
                pltpu.make_async_copy(
                    refs[source].at[pl.ds(start, rows)], outs[out].at[pl.ds(first, rows)], sem.at[step]
                ).start()
    for step, (out, first, rows, _, options) in enumerate(plan):
        source, start = next(iter(options.values()))
        pltpu.make_async_copy(
            refs[source].at[pl.ds(start, rows)], outs[out].at[pl.ds(first, rows)], sem.at[step]
        ).wait()


def assembled(at, sources, plan, out_rows):
    width = sources[0].shape[1]
    return pl.pallas_call(
        functools.partial(assemble_kernel, plan, len(sources)),
        grid_spec=pltpu.PrefetchScalarGridSpec(
            num_scalar_prefetch=1,
            grid=(1,),
            in_specs=[pl.BlockSpec(memory_space=pl.ANY)] * len(sources),
            out_specs=[pl.BlockSpec((rows, width), lambda i, at: (0, 0)) for rows in out_rows],
            scratch_shapes=[pltpu.SemaphoreType.DMA((len(plan),))],
        ),
        out_shape=[jax.ShapeDtypeStruct((rows, width), jnp.bfloat16) for rows in out_rows],
        compiler_params=pltpu.CompilerParams(vmem_limit_bytes=VMEM_LIMIT),
        cost_estimate=SMALL,
    )(at, *sources)


def base_kernel(blocks, target_ref, own_ref, place_ref, front_ref, factor_ref, col_ref, given_ref, out_ref):
    factor = factor_ref[...]
    for block in range(blocks):
        here = pl.ds(block * BLK, BLK)
        own = pl.ds(pl.multiple_of(place_ref[block] * BLK, BLK), BLK)
        product = lax.dot_general(factor, col_ref[own, :], NT, preferred_element_type=jnp.float32)
        kept = (front_ref[:, own].astype(jnp.float32) - product).astype(jnp.bfloat16)
        out_ref[:, here] = given_ref[:, here].astype(jnp.float32) + kept.astype(jnp.float32)


def kept_rows(targets, owns, places, front, factor, col_side, given):
    count = targets.shape[0]
    cols = front.shape[1]
    pivots = factor.shape[1]
    return pl.pallas_call(
        functools.partial(base_kernel, cols // BLK),
        grid_spec=pltpu.PrefetchScalarGridSpec(
            num_scalar_prefetch=3,
            grid=(count,),
            in_specs=[
                pl.BlockSpec((BLK, cols), lambda i, targets, owns, places: (owns[i], 0)),
                pl.BlockSpec((BLK, pivots), lambda i, targets, owns, places: (owns[i], 0)),
                pl.BlockSpec(col_side.shape, lambda i, targets, owns, places: (0, 0)),
                pl.BlockSpec((BLK, cols), lambda i, targets, owns, places: (targets[i], 0)),
            ],
            out_specs=pl.BlockSpec((BLK, cols), lambda i, targets, owns, places: (targets[i], 0)),
        ),
        out_shape=jax.ShapeDtypeStruct(given.shape, jnp.float32),
        compiler_params=pltpu.CompilerParams(vmem_limit_bytes=VMEM_LIMIT),
        cost_estimate=SMALL,
    )(targets, owns, places, front, factor, col_side, given)


def add_kernel(blocks, pieces, target_ref, place_ref, *refs):
    piece_refs, base_ref, out_ref = refs[:pieces], refs[-2], refs[-1]
    for block in range(blocks):
        here = pl.ds(block * BLK, BLK)
        arrived = piece_refs[0][:, pl.ds(pl.multiple_of(place_ref[0, block] * BLK, BLK), BLK)]
        if pieces == 2:
            other = piece_refs[1][:, pl.ds(pl.multiple_of(place_ref[1, block] * BLK, BLK), BLK)]
            arrived = jnp.where(place_ref[2, block] == 0, arrived, other)
        out_ref[:, here] = base_ref[:, here] + arrived.astype(jnp.float32)


def add_rows(base, targets, places, pieces, first=0):
    parts = BLK // STEP
    skip = first // STEP
    count = pieces[0].shape[0] // STEP
    cols = base.shape[1]
    row = pl.BlockSpec(
        (STEP, cols),
        lambda i, targets, places: (targets[(i + skip) // parts] * parts + (i + skip) % parts, 0),
    )
    in_specs = [pl.BlockSpec((STEP, piece.shape[1]), lambda i, *_: (i, 0)) for piece in pieces]
    return pl.pallas_call(
        functools.partial(add_kernel, cols // BLK, len(pieces)),
        grid_spec=pltpu.PrefetchScalarGridSpec(
            num_scalar_prefetch=2, grid=(count,), in_specs=in_specs + [row], out_specs=row
        ),
        out_shape=jax.ShapeDtypeStruct(base.shape, jnp.float32),
        input_output_aliases={2 + len(pieces): 0},
        compiler_params=pltpu.CompilerParams(vmem_limit_bytes=VMEM_LIMIT),
        cost_estimate=SMALL,
    )(targets, places, *pieces, base)


def take_block(table, first, count):
    return lax.dynamic_slice_in_dim(table, first, count, 0)


def hop(up_block, down_block, up, down):
    return lax.ppermute(up_block, "col", up), lax.ppermute(down_block, "col", down)


UP = [(0, 1), (1, 2), (2, 3)]
DOWN = [(1, 0), (2, 1), (3, 2)]
FAR = [(2, 3), (1, 0)]


def other_core(block):
    return lax.ppermute(block, "row", [(0, 1), (1, 0)])


def segment_at(segment, at_ref):
    away = segment - at_ref[0]
    far = jnp.where(away == 2, 4, 5)
    near = jnp.where(away == -1, 1, jnp.where(away == 1, 2, jnp.where(away == -2, 3, far)))
    return jnp.where(away == 0, 0, near)


def col_pieces(at, sources):
    size = sources[0].shape[0]
    half = size // 2
    plan = []
    for index in range(4):
        segment = index // 2
        choice = functools.partial(lambda segment, at_ref: segment_at(at_ref[0] % 2 * 2 + segment, at_ref), segment)
        plan.append((index, 0, half, choice, {k: (k, index % 2 * half) for k in range(5)}))
    return plan, [half] * 4


def owned_cols(at, pieces, swapped):
    size = pieces[0].shape[0]
    plan = [
        (0, i * size, size, lambda at_ref: jnp.where(at_ref[1] == at_ref[0] // 2, 0, 1), {0: (i, 0), 1: (4 + i, 0)})
        for i in range(4)
    ]
    return assembled(at, [*pieces, *swapped], plan, [4 * size])[0]


def factor_of(panel, inverse, fill, first_row):
    local_rows = panel.shape[0]
    positions = (first_row + jnp.arange(local_rows, dtype=jnp.int32)) // BLK
    blocks = jnp.arange(fill.shape[0], dtype=jnp.int32)
    row_fill = jnp.sum(
        (positions[:, None] == blocks[None, :]).astype(jnp.int32) * fill[None, :], axis=1
    )
    masked = panel * row_fill[:, None].astype(jnp.bfloat16)
    return jnp.dot(masked, jnp.triu(inverse), preferred_element_type=jnp.float32).astype(jnp.bfloat16)


def from_sibling(block):
    route = []
    for low in range(0, lax.axis_size("front"), 2):
        route += [(low, low + 1), (low + 1, low)]
    return lax.ppermute(block, "front", route)


def shards(front, panel, inverse, fill, block_map, parent_front):
    front, panel, given = front[0], panel[0], parent_front[0]
    col_count = lax.axis_size("col")
    row_count = lax.axis_size("row")
    core = lax.axis_index("row")
    place = lax.axis_index("col")
    parity = lax.axis_index("front") % 2
    local_rows = panel.shape[0]
    tile_rows, tile_cols = front.shape
    half_blocks = tile_rows // 2 // BLK
    col_blocks = tile_cols // BLK
    seg = local_rows // BLK
    row_base = core * (tile_rows // BLK)
    sibling_map = from_sibling(block_map[0])
    source = block_inverse(block_map[0])
    col_source = take_block(source, place * col_blocks, col_blocks) - place * col_blocks
    first_row = (core * col_count + place) * local_rows

    closed = half_blocks % col_blocks == 0
    line = (
        row_count == 2 and col_count == 4 and closed and tile_rows == 2 * tile_cols
        and local_rows % (2 * BLK) == 0 and 2 * local_rows == tile_cols
    )
    if not line:
        factor = factor_of(panel, inverse[0], fill[0], first_row)
        all_rows = lax.all_gather(factor, ("row", "col"), axis=0, tiled=True)
        row_side = take_block(all_rows, core * tile_rows, tile_rows)
        col_side = take_block(all_rows, place * tile_cols, tile_cols)
        sent = take_block(source, row_base + (1 - parity) * half_blocks, half_blocks) - row_base
        owns = take_block(source, row_base + parity * half_blocks, half_blocks) - row_base
        targets = jnp.arange(half_blocks, dtype=jnp.int32)
        grid = (half_blocks, 1)
        arrived = from_sibling(updated_rows(
            front, sent, lambda i, at: at[i], row_side, lambda i, at: at[i], col_side, grid, BLK,
            tile_cols, 1, 0,
        ))
        sibling_cols = take_block(block_inverse(sibling_map), place * col_blocks, col_blocks)
        sibling_cols = sibling_cols - place * col_blocks
        base = kept_rows(targets, owns, col_source, front, row_side, col_side, given)
        out = add_rows(base, targets, sibling_cols[None], [arrived])
        return factor[None], out[None]

    cut = seg // 2
    unit = cut * BLK
    parts = BLK // STEP
    at = jnp.stack([place, core, parity]).astype(jnp.int32)
    after = lax.optimization_barrier

    def sent_row(inner, per_block):
        def row(at):
            sent = 1 - at[2]
            return (sent * half_blocks + (at[2] if inner else sent) * seg) * per_block
        return row

    def raw_row(first):
        def row(i, at):
            index = i + first
            in_cut = cut * parts
            inner = index < in_cut
            start = jnp.where(inner, sent_row(True, parts)(at), sent_row(False, parts)(at))
            return start + index - jnp.where(inner, 0, in_cut)
        return row

    raw = [
        picked_rows(front, at, raw_row(first), (count, 2), STEP, unit, 2) for first, count in RAW_PIECES
    ]
    raw[0] = from_sibling(raw[0])
    raw[1] = from_sibling(raw[1])
    factor = factor_of(panel, inverse[0], fill[0], first_row)
    factor, raw[0], sibling_map = after((factor, raw[0], sibling_map))
    below, above = hop(factor, factor, UP, DOWN)
    raw[2] = from_sibling(raw[2])
    below, above, raw[1] = after((below, above, raw[1]))
    below2, above2 = hop(below, above, UP[1:], DOWN[:2])
    raw[3] = jnp.concatenate([raw[3], factor[:unit].reshape(-1, raw[3].shape[1])], axis=0)
    raw[3] = from_sibling(raw[3])
    at2, raw[2] = after((at, raw[2]))
    near = [factor, below, above, below2, above2]
    plan, sizes = col_pieces(at2, near)
    plan.append((
        4, 0, local_rows, lambda at_ref: segment_at(jnp.where(at_ref[2] == 1, 1, 2), at_ref),
        {k: (k, 0) for k in range(5)},
    ))
    *pieces, inner_rows = assembled(at2, near, plan, sizes + [local_rows])
    col_side = owned_cols(at, pieces, [other_core(piece) for piece in pieces])
    far = lax.ppermute(jnp.where(place == 2, below2, above2), "col", FAR)

    def contribution(at, inner, first, rows, kind_x, factor):
        height = min(rows, BLK)
        start = sent_row(inner, BLK // height)
        skip = first // height
        grid, layout = ((rows // height, 2), (2, 1)) if kind_x else ((rows // height, 4), (1, 0))
        return from_sibling(updated_rows(
            front, at, lambda i, at: start(at) + skip + i, factor,
            lambda i, at: i + skip if inner else start(at) + skip + i, col_side, grid, height, unit, *layout,
        ))

    arrived = [contribution(at, True, 0, unit, True, inner_rows)]
    for i in range(cut):
        at_i = at
        if i == 0:
            raw[3], sibling_map = after((raw[3], sibling_map))
            at_i, sibling_map = after((at, other_core(sibling_map)))
        elif i == 2:
            at_i, arrived[0] = after((at, arrived[0]))
        arrived.append(contribution(at_i, True, unit + i * BLK, BLK, False, inner_rows))
    plan = [
        (0, k * local_rows, local_rows, functools.partial(segment_at, k), {j: (j, 0) for j in range(6)})
        for k in range(4)
    ]
    far, arrived[1] = after((far, arrived[1]))
    row_side = assembled(at, [*near, far], plan, [tile_rows])[0]
    arrived.append(contribution(at, False, 0, unit, True, row_side))

    sibling_part = raw[3][RAW_PIECES[3][1] * STEP:].reshape(unit, -1)
    raw[3] = raw[3][:RAW_PIECES[3][1] * STEP]
    part_below, part_above = hop(sibling_part, sibling_part, UP, DOWN)
    part_below, part_above, arrived[0] = after((part_below, part_above, arrived[0]))
    part_below2, part_above2 = hop(part_below, part_above, UP[1:], DOWN[:2])
    part_far = lax.ppermute(jnp.where(place == 2, part_below2, part_above2), "col", FAR)
    parts_near = [sibling_part, part_below, part_above, part_below2, part_above2]
    plan, sizes = col_pieces(at, parts_near)
    part_pieces = assembled(at, parts_near, plan, sizes)
    sibling_col = owned_cols(at, part_pieces, [other_core(piece) for piece in part_pieces])
    plan = [
        (0, k * unit, unit, functools.partial(
            lambda k, at_ref: segment_at(jnp.where(at_ref[2] == 0, 1 - k, 2 + k), at_ref), k
        ), {j: (j, 0) for j in range(6)})
        for k in range(2)
    ]
    part_rows = assembled(at, [*parts_near, part_far], plan, [2 * unit])[0]
    finished = updated_rows(
        jnp.concatenate(raw, axis=0), at, lambda i, at: i, part_rows, lambda i, at: i, sibling_col,
        (2 * cut, 2), BLK, unit, 1, 0,
    )

    kept_base = row_base + parity * half_blocks
    owns = take_block(source, kept_base, half_blocks) - row_base
    base = kept_rows(
        jnp.arange(half_blocks, dtype=jnp.int32), owns, col_source, front, row_side, col_side, given
    )
    sibling_cols = take_block(block_inverse(sibling_map), place * col_blocks, col_blocks)
    sibling_cols = sibling_cols - place * col_blocks
    landed = take_block(sibling_map, kept_base, half_blocks) - kept_base
    seg_at = sibling_cols // seg * cut
    seg_in = sibling_cols % seg
    places_x = jnp.stack([
        seg_at + jnp.minimum(seg_in, cut - 1),
        seg_at + jnp.maximum(seg_in - cut, 0),
        jnp.where(seg_in < cut, 0, 1),
    ])
    places_y = sibling_cols[None]
    kept_inner = (1 - parity) * seg
    kept_outer = seg - kept_inner

    def add(out, index):
        start = kept_inner if index <= cut else kept_outer
        which = index % (1 + cut)
        if which == 0:
            now = finished[:unit] if index == 0 else finished[unit:]
            return add_rows(out, take_block(landed, start, cut), places_x, [now, arrived[index]])
        targets = take_block(landed, start + cut + which - 1, 1)
        if isinstance(arrived[index], list):
            for piece, first in arrived[index]:
                out = add_rows(out, targets, places_y, [piece], first)
            return out
        return add_rows(out, targets, places_y, [arrived[index]])

    out, added = base, 0
    for i in range(cut):
        at_i, arrived[2 + i], out = after((at, arrived[2 + i], out))
        first = unit + i * BLK
        if i < cut - 1:
            arrived.append(contribution(at_i, False, first, BLK, False, row_side))
        else:
            arrived.append([
                (contribution(at_i, False, first + k, STEP, False, row_side), k) for k in range(0, BLK, STEP)
            ])
        for _ in range(2):
            out = add(out, added)
            added += 1
    while added < len(arrived):
        out = add(out, added)
        added += 1
    return factor[None], out[None]


def solution(mesh):
    placed = (
        P("front", "row", "col"),
        P("front", ("row", "col"), None),
        P("front", None, None),
        P("front", None),
        P("front", None),
        P("front", "row", "col"),
    )
    return jax.shard_map(
        shards,
        mesh=mesh,
        in_specs=placed,
        out_specs=(P("front", ("row", "col"), None), P("front", "row", "col")),
        check_vma=False,
    )
```

```python
import functools

import jax
import jax.numpy as jnp
from jax import lax
from jax.experimental import pallas as pl
from jax.experimental.pallas import tpu as pltpu
from jax.sharding import PartitionSpec as P

BLK = 256
NT = (((1,), (1,)), ((), ()))
VMEM_LIMIT = 48 * 1024 * 1024
STEP = 128
MAP_ROWS = 16


def block_inverse(mapping):
    block_total = mapping.shape[0]
    target = jnp.arange(block_total, dtype=jnp.int32)
    matches = (mapping[:, None] == target[None, :]).astype(jnp.int32)
    return jnp.sum(matches * target[:, None], axis=0)


SMALL = pl.CostEstimate(flops=1, bytes_accessed=1, transcendentals=0)


def update_kernel(unit, col_unit, at_ref, front_ref, factor_ref, col_ref, out_ref):
    first = col_unit(pl.program_id(1)) * unit
    col = col_ref[pl.ds(pl.multiple_of(first, unit), unit), :]
    product = lax.dot_general(factor_ref[...], col, NT, preferred_element_type=jnp.float32)
    out_ref[...] = (front_ref[...].astype(jnp.float32) - product).astype(jnp.bfloat16)


def updated_rows(front, at, front_row, front_col, factor, factor_row, col_side, col_unit, grid, height, unit):
    pivots = factor.shape[1]
    return pl.pallas_call(
        functools.partial(update_kernel, unit, col_unit),
        grid_spec=pltpu.PrefetchScalarGridSpec(
            num_scalar_prefetch=1,
            grid=grid,
            in_specs=[
                pl.BlockSpec((height, unit), lambda i, j, at: (front_row(i, at), front_col(j, at))),
                pl.BlockSpec((height, pivots), lambda i, j, at: (factor_row(i, at), 0)),
                pl.BlockSpec(col_side.shape, lambda i, j, at: (0, 0)),
            ],
            out_specs=pl.BlockSpec((height, unit), lambda i, j, at: (i, j)),
        ),
        out_shape=jax.ShapeDtypeStruct((grid[0] * height, grid[1] * unit), jnp.bfloat16),
        compiler_params=pltpu.CompilerParams(vmem_limit_bytes=VMEM_LIMIT),
        cost_estimate=SMALL,
    )(at, front, factor, col_side)


def pick_kernel(at_ref, front_ref, out_ref):
    out_ref[...] = front_ref[...]


def picked_rows(front, at, first_row, rows, unit, stride, offset):
    units = front.shape[1] // unit // stride
    return pl.pallas_call(
        pick_kernel,
        grid_spec=pltpu.PrefetchScalarGridSpec(
            num_scalar_prefetch=1,
            grid=(units,),
            in_specs=[pl.BlockSpec(
                (pl.Element(rows), pl.Element(unit)),
                lambda j, at: (first_row(0, at), (j * stride + offset) * unit),
            )],
            out_specs=pl.BlockSpec((rows, unit), lambda j, at: (0, j)),
        ),
        out_shape=jax.ShapeDtypeStruct((rows, units * unit), jnp.bfloat16),
        compiler_params=pltpu.CompilerParams(vmem_limit_bytes=VMEM_LIMIT),
        cost_estimate=SMALL,
    )(at, front)


def assemble_kernel(plan, sources, at_ref, *refs):
    outs, sem = refs[sources:-1], refs[-1]
    for step, (out, first, rows, choice, options) in enumerate(plan):
        chosen = choice(at_ref)
        for value, (source, start) in options.items():
            @pl.when(chosen == value)
            def _():
                pltpu.make_async_copy(
                    refs[source].at[pl.ds(start, rows)], outs[out].at[pl.ds(first, rows)], sem.at[step]
                ).start()
    for step, (out, first, rows, _, options) in enumerate(plan):
        source, start = next(iter(options.values()))
        pltpu.make_async_copy(
            refs[source].at[pl.ds(start, rows)], outs[out].at[pl.ds(first, rows)], sem.at[step]
        ).wait()


def assembled(at, sources, plan, out_rows):
    width = sources[0].shape[1]
    return pl.pallas_call(
        functools.partial(assemble_kernel, plan, len(sources)),
        grid_spec=pltpu.PrefetchScalarGridSpec(
            num_scalar_prefetch=1,
            grid=(1,),
            in_specs=[pl.BlockSpec(memory_space=pl.ANY)] * len(sources),
            out_specs=[pl.BlockSpec((rows, width), lambda i, at: (0, 0)) for rows in out_rows],
            scratch_shapes=[pltpu.SemaphoreType.DMA((len(plan),))],
        ),
        out_shape=[jax.ShapeDtypeStruct((rows, width), jnp.bfloat16) for rows in out_rows],
        compiler_params=pltpu.CompilerParams(vmem_limit_bytes=VMEM_LIMIT),
        cost_estimate=SMALL,
    )(at, *sources)


def base_kernel(blocks, target_ref, own_ref, place_ref, front_ref, factor_ref, col_ref, given_ref, out_ref):
    factor = factor_ref[...]
    for block in range(blocks):
        here = pl.ds(block * BLK, BLK)
        own = pl.ds(pl.multiple_of(place_ref[block] * BLK, BLK), BLK)
        product = lax.dot_general(factor, col_ref[own, :], NT, preferred_element_type=jnp.float32)
        kept = (front_ref[:, own].astype(jnp.float32) - product).astype(jnp.bfloat16)
        out_ref[:, here] = given_ref[:, here].astype(jnp.float32) + kept.astype(jnp.float32)


def kept_rows(targets, owns, places, front, factor, col_side, given):
    count = targets.shape[0]
    cols = front.shape[1]
    pivots = factor.shape[1]
    return pl.pallas_call(
        functools.partial(base_kernel, cols // BLK),
        grid_spec=pltpu.PrefetchScalarGridSpec(
            num_scalar_prefetch=3,
            grid=(count,),
            in_specs=[
                pl.BlockSpec((BLK, cols), lambda i, targets, owns, places: (owns[i], 0)),
                pl.BlockSpec((BLK, pivots), lambda i, targets, owns, places: (owns[i], 0)),
                pl.BlockSpec(col_side.shape, lambda i, targets, owns, places: (0, 0)),
                pl.BlockSpec((BLK, cols), lambda i, targets, owns, places: (targets[i], 0)),
            ],
            out_specs=pl.BlockSpec((BLK, cols), lambda i, targets, owns, places: (targets[i], 0)),
        ),
        out_shape=jax.ShapeDtypeStruct(given.shape, jnp.float32),
        compiler_params=pltpu.CompilerParams(vmem_limit_bytes=VMEM_LIMIT),
        cost_estimate=SMALL,
    )(targets, owns, places, front, factor, col_side, given)


def add_kernel(blocks, pieces, target_ref, place_ref, *refs):
    base_ref, out_ref = refs[-2], refs[-1]
    for block in range(blocks):
        here = pl.ds(block * BLK, BLK)
        arrived = None
        for k in range(pieces):
            part = refs[k][:, pl.ds(pl.multiple_of(place_ref[1 + k, block] * BLK, BLK), BLK)]
            arrived = part if arrived is None else jnp.where(place_ref[0, block] == k, part, arrived)
        out_ref[:, here] = base_ref[:, here] + arrived.astype(jnp.float32)


def add_rows(base, targets, places, pieces, count, step=STEP, first=0):
    parts = BLK // step
    skip = first // step
    cols = base.shape[1]
    row = pl.BlockSpec(
        (step, cols),
        lambda i, targets, places: (targets[(i + skip) // parts] * parts + (i + skip) % parts, 0),
    )
    in_specs = [
        pl.BlockSpec((step, piece.shape[1]), functools.partial(lambda begin, i, *_: (i + begin, 0), begin // step))
        for piece, begin in pieces
    ]
    return pl.pallas_call(
        functools.partial(add_kernel, cols // BLK, len(pieces)),
        grid_spec=pltpu.PrefetchScalarGridSpec(
            num_scalar_prefetch=2, grid=(count // step,), in_specs=in_specs + [row], out_specs=row
        ),
        out_shape=jax.ShapeDtypeStruct(base.shape, jnp.float32),
        input_output_aliases={2 + len(pieces): 0},
        compiler_params=pltpu.CompilerParams(vmem_limit_bytes=VMEM_LIMIT),
        cost_estimate=SMALL,
    )(targets, places, *(piece for piece, _ in pieces), base)


def take_block(table, first, count):
    return lax.dynamic_slice_in_dim(table, first, count, 0)


def hop(up_block, down_block, up, down):
    return lax.ppermute(up_block, "col", up), lax.ppermute(down_block, "col", down)


UP = [(0, 1), (1, 2), (2, 3)]
DOWN = [(1, 0), (2, 1), (3, 2)]
FAR = [(2, 3), (1, 0)]


def other_core(block):
    return lax.ppermute(block, "row", [(0, 1), (1, 0)])


def segment_at(segment, at_ref):
    away = segment - at_ref[0]
    far = jnp.where(away == 2, 4, 5)
    near = jnp.where(away == -1, 1, jnp.where(away == 1, 2, jnp.where(away == -2, 3, far)))
    return jnp.where(away == 0, 0, near)


def settled(array, table, turns):
    array, table = lax.optimization_barrier((array, table))
    for _ in range(turns):
        table = other_core(table)
    return array, table


def near_source(at_ref):
    own = segment_at(col_segment(False)(at_ref), at_ref)
    other = jnp.where((at_ref[0] == 1) | (at_ref[0] == 2), 3, 4)
    return jnp.where(not_owner(at_ref) == 0, own, other)


def options(sources, rows=0):
    return {k: (k, rows) for k in range(sources)}


def col_segment(far):
    def segment(at_ref):
        low = at_ref[0] % 2 * 2
        near = at_ref[0] // 2
        return low + (1 - near if far else near)
    return segment


def inner_segment(at_ref):
    return jnp.where(at_ref[2] == 1, 1, 2)


def at_segment(segment):
    return lambda at_ref: segment_at(segment(at_ref), at_ref)


def not_owner(at_ref):
    return jnp.where(at_ref[1] == at_ref[0] // 2, 0, 1)


def factor_of(panel, inverse, fill, first_row):
    local_rows = panel.shape[0]
    positions = (first_row + jnp.arange(local_rows, dtype=jnp.int32)) // BLK
    blocks = jnp.arange(fill.shape[0], dtype=jnp.int32)
    row_fill = jnp.sum(
        (positions[:, None] == blocks[None, :]).astype(jnp.int32) * fill[None, :], axis=1
    )
    masked = panel * row_fill[:, None].astype(jnp.bfloat16)
    return jnp.dot(masked, jnp.triu(inverse), preferred_element_type=jnp.float32).astype(jnp.bfloat16)


def from_sibling(block):
    route = []
    for low in range(0, lax.axis_size("front"), 2):
        route += [(low, low + 1), (low + 1, low)]
    return lax.ppermute(block, "front", route)


def shards(front, panel, inverse, fill, block_map, parent_front):
    front, panel, given = front[0], panel[0], parent_front[0]
    col_count = lax.axis_size("col")
    row_count = lax.axis_size("row")
    core = lax.axis_index("row")
    place = lax.axis_index("col")
    parity = lax.axis_index("front") % 2
    local_rows = panel.shape[0]
    tile_rows, tile_cols = front.shape
    half_blocks = tile_rows // 2 // BLK
    col_blocks = tile_cols // BLK
    seg = local_rows // BLK
    row_base = core * (tile_rows // BLK)
    source = block_inverse(block_map[0])
    col_source = take_block(source, place * col_blocks, col_blocks) - place * col_blocks
    first_row = (core * col_count + place) * local_rows

    closed = half_blocks % col_blocks == 0
    line = (
        row_count == 2 and col_count == 4 and closed and tile_rows == 2 * tile_cols
        and local_rows == 6 * BLK and 2 * local_rows == tile_cols
    )
    if not line:
        sibling_map = from_sibling(block_map[0])
        factor = factor_of(panel, inverse[0], fill[0], first_row)
        all_rows = lax.all_gather(factor, ("row", "col"), axis=0, tiled=True)
        row_side = take_block(all_rows, core * tile_rows, tile_rows)
        col_side = take_block(all_rows, place * tile_cols, tile_cols)
        sent = take_block(source, row_base + (1 - parity) * half_blocks, half_blocks) - row_base
        owns = take_block(source, row_base + parity * half_blocks, half_blocks) - row_base
        targets = jnp.arange(half_blocks, dtype=jnp.int32)
        grid = (half_blocks, 1)
        arrived = from_sibling(updated_rows(
            front, sent, lambda i, at: at[i], lambda j, at: j, row_side, lambda i, at: at[i], col_side,
            lambda j: j, grid, BLK, tile_cols,
        ))
        sibling_cols = take_block(block_inverse(sibling_map), place * col_blocks, col_blocks)
        sibling_cols = sibling_cols - place * col_blocks
        base = kept_rows(targets, owns, col_source, front, row_side, col_side, given)
        places = jnp.stack([jnp.zeros_like(sibling_cols), sibling_cols])
        out = add_rows(base, targets, places, [(arrived, 0)], half_blocks * BLK)
        return factor[None], out[None]

    half = local_rows // 2
    cut = local_rows * 3 // 8
    thin = local_rows // 8
    wide = local_rows // 3
    at = jnp.stack([place, core, parity]).astype(jnp.int32)
    after = lax.optimization_barrier

    def sent_row(inner, height):
        def row(at):
            sent = 1 - at[2]
            return sent * (half_blocks * BLK // height) + (at[2] if inner else sent) * (local_rows // height)
        return row

    def raw_rows(inner, first, rows):
        start = sent_row(inner, thin)
        skip = (local_rows - cut + first) // thin
        return picked_rows(front, at, lambda i, at: (start(at) + skip) * thin, rows, wide, 3, 2)

    raw = [raw_rows(*piece) for piece in ((True, 0, cut - thin), (False, 0, cut), (True, cut - thin, thin))]
    panel, raw[0] = after((panel, raw[0]))
    factor_a = factor_of(panel[:half], inverse[0], fill[0], first_row)
    raw[0] = from_sibling(raw[0])
    below_a, above_a = hop(factor_a, factor_a, UP, DOWN)
    factor_b = factor_of(panel[half:], inverse[0], fill[0], first_row + half)
    raw[1] = from_sibling(raw[1])
    near_part = assembled(
        at, [factor_a, below_a, above_a], [(0, 0, half, at_segment(col_segment(False)), options(3))], [half]
    )[0]
    near_other = other_core(near_part)
    raw[0], own_map = settled(raw[0], block_map[0], 1)
    below_a, above_a, own_map = after((below_a, above_a, own_map))
    below2_a, above2_a = hop(below_a, above_a, UP[1:], DOWN[:2])
    width = raw[2].shape[1]
    map_rows = jnp.pad(block_map[0].astype(jnp.bfloat16), (0, width - block_map.shape[1]))
    map_rows = jnp.broadcast_to(map_rows[None], (MAP_ROWS, width))
    part = factor_b[half - cut:].reshape(-1, width)
    raw[2] = jnp.concatenate([raw[2], part, map_rows], axis=0)
    raw[2] = from_sibling(raw[2])
    raw[1], own_map = settled(raw[1], own_map, 1)
    at_a, own_map = after((at, own_map))
    sources_a = [factor_a, below_a, above_a, below2_a, above2_a]
    near_a = assembled(
        at, [near_part, near_other], [(0, 0, half, not_owner, {0: (0, 0), 1: (1, 0)})], [half]
    )[0]
    inner_a = assembled(at_a, sources_a, [(0, 0, half, at_segment(inner_segment), options(5))], [half])[0]

    arrived = []

    def contribution(at, inner, first, rows, factor, factor_first, col_side, unit, units, front_col, col_unit):
        height = thin if rows % thin == 0 else min(rows, BLK)
        start = sent_row(inner, height)
        piece = updated_rows(
            front, at, lambda i, at: start(at) + first // height + i, front_col, factor,
            lambda i, at: factor_first(at, height) + i, col_side, col_unit, (rows // height, units), height, unit,
        )
        return piece

    def quarter(at, col_side, far, second):
        def front_col(j, at):
            near = at[0] // 2
            return (1 - near if far else near) * 2 + second
        return contribution(
            at, True, 0, half, inner_a, lambda at, height: 0, col_side, half, 1, front_col, lambda j: 0
        )

    piece = quarter(at_a, near_a, False, 0)
    at_f, piece = after((at_a, piece))
    arrived.append(from_sibling(piece))
    far_part = assembled(
        at_f, sources_a, [(0, 0, half, at_segment(col_segment(True)), options(5))], [half]
    )[0]
    far_a = assembled(
        at, [far_part, other_core(far_part)], [(0, 0, half, not_owner, {0: (0, 0), 1: (1, 0)})], [half]
    )[0]

    raw[2], own_map = settled(raw[2], own_map, 1)
    later, far_a, own_map, own_other = after((factor_b, far_a, own_map, other_core(factor_b)))
    arrived.append(from_sibling(quarter(at, far_a, True, 0)))
    below_b, above_b = hop(later, later, UP, DOWN)
    cross = lax.ppermute(later, ("row", "col"), [(2, col_count + 1), (col_count + 1, 2)])
    arrived[0], own_map = settled(arrived[0], own_map, 2)
    below_b, above_b, cross, own_map = after((below_b, above_b, cross, own_map))
    near_b = assembled(at, [factor_b, below_b, above_b, cross, own_other], [
        (0, 0, half, near_source, options(5))
    ], [half])[0]
    below2_b, above2_b = hop(below_b, above_b, UP[1:], DOWN[:2])
    arrived.append(from_sibling(quarter(at, near_b, False, 1)))
    sources_b = [factor_b, below_b, above_b, below2_b, above2_b]
    second = options(5)
    inner_b, far_part = assembled(at, sources_b, [
        (0, 0, half, at_segment(inner_segment), second),
        (1, 0, half, at_segment(col_segment(True)), second),
    ], [half] * 2)
    arrived[1], own_map = settled(arrived[1], own_map, 3)
    far_part, own_map = after((far_part, own_map))
    far_b = assembled(
        at, [far_part, other_core(far_part)], [(0, 0, half, not_owner, {0: (0, 0), 1: (1, 0)})], [half]
    )[0]
    arrived.append(from_sibling(quarter(at, far_b, True, 1)))
    col_side = assembled(at, [near_a, far_a, near_b, far_b], [
        (0, (2 * segment + k) * half, half, functools.partial(
            lambda segment, at_ref: jnp.where(at_ref[0] // 2 == segment, 0, 1), segment
        ), {0: (2 * k, 0), 1: (2 * k + 1, 0)})
        for segment in range(2) for k in range(2)
    ], [tile_cols])[0]

    def whole_row(at, inner, first, rows, factor, factor_first):
        arrived.append(from_sibling(contribution(
            at, inner, first, rows, factor, factor_first, col_side, half, 4, lambda j, at: j, lambda j: j
        )))

    def cut_rows(at, inner, factor, factor_first):
        arrived.append(from_sibling(contribution(
            at, inner, local_rows - cut, cut, factor, factor_first, col_side, wide, 4,
            lambda j, at: j + j // 2, lambda j: j + j // 2,
        )))

    arrived[2], own_map = settled(arrived[2], own_map, 1)
    at_i, own_map = after((at, own_map))
    cut_rows(at_i, True, inner_b, lambda at, height: 1)
    arrived[3], turned = settled(arrived[3], inner_b[:576], 2)
    whole_row(at, True, half, thin, turned, lambda at, height: 0)

    last_hop = assembled(at, [below2_a, above2_a, below2_b, above2_b], [
        (0, k * half, half, lambda at_ref: jnp.where(at_ref[0] == 2, 0, 1), {0: (2 * k, 0), 1: (2 * k + 1, 0)})
        for k in range(2)
    ], [local_rows])[0]
    last_hop, arrived[1] = after((last_hop, arrived[1]))
    far = lax.ppermute(last_hop, "col", FAR)
    row_side = assembled(at, [*sources_a, *sources_b, far], [
        (0, (2 * segment + k) * half, half, functools.partial(segment_at, segment), {
            **{j: (j + 5 * k, 0) for j in range(5)}, 5: (10, k * half)
        })
        for segment in range(4) for k in range(2)
    ], [tile_rows])[0]

    def outer_row(first):
        return lambda at, height: sent_row(False, height)(at) + first // height

    at_i, arrived[4] = after((at, arrived[4]))
    whole_row(at_i, False, 0, BLK, row_side, outer_row(0))

    sibling_map = raw[2][-1, :block_map.shape[1]].astype(jnp.int32)
    part = raw[2][thin:-MAP_ROWS].reshape(cut, -1)
    raw[2] = raw[2][:thin]
    part_below, part_above = hop(part, part, UP, DOWN)
    part_below, part_above, arrived[3] = after((part_below, part_above, arrived[3]))
    part_below2, part_above2 = hop(part_below, part_above, UP[1:], DOWN[:2])
    part_far = lax.ppermute(jnp.where(place == 2, part_below2, part_above2), "col", FAR)
    parts_near = [part, part_below, part_above, part_below2, part_above2]
    part_cols = assembled(at, parts_near, [
        (k, 0, wide, functools.partial(lambda k, at_ref: segment_at(at_ref[0] % 2 * 2 + k, at_ref), k),
         options(5, cut - wide))
        for k in range(2)
    ], [wide] * 2)
    others = [other_core(piece) for piece in part_cols]
    sibling_col = assembled(at, [*part_cols, *others], [
        (0, k * wide, wide, not_owner, {0: (k, 0), 1: (2 + k, 0)}) for k in range(2)
    ], [2 * wide])[0]
    part_rows = assembled(at, [*parts_near, part_far], [
        (0, k * cut, cut, functools.partial(
            lambda k, at_ref: segment_at(jnp.where(at_ref[2] == 0, 1 - k, 2 + k), at_ref), k
        ), options(6))
        for k in range(2)
    ], [2 * cut])[0]
    finished = updated_rows(
        jnp.concatenate([raw[0], raw[2], raw[1]], axis=0), at, lambda i, at: i, lambda j, at: j, part_rows, lambda i, at: i, sibling_col,
        lambda j: j, (2 * cut // thin, 2), thin, wide,
    )

    kept_base = row_base + parity * half_blocks
    source = block_inverse(own_map)
    owns = take_block(source, kept_base, half_blocks) - row_base
    col_source = take_block(source, place * col_blocks, col_blocks) - place * col_blocks
    base = kept_rows(
        jnp.arange(half_blocks, dtype=jnp.int32), owns, col_source, front, row_side, col_side, given
    )
    sibling_cols = take_block(block_inverse(sibling_map), place * col_blocks, col_blocks)
    sibling_cols = sibling_cols - place * col_blocks
    landed = take_block(sibling_map, kept_base, half_blocks) - kept_base
    segment, within = sibling_cols // seg, sibling_cols % seg
    cut_blocks = wide // BLK
    cut_first = seg - cut_blocks
    is_far = jnp.where(segment == place // 2, 0, 1)
    quarter_at = within % (seg // 2)
    places_q = jnp.stack([within // (seg // 2) * 2 + is_far] + [quarter_at] * 4)
    places_w = jnp.stack([jnp.zeros_like(sibling_cols), sibling_cols])
    places_c = jnp.stack([
        jnp.where(within < cut_first, 1, 0),
        segment * cut_blocks + jnp.maximum(within - cut_first, 0),
        segment * cut_first + jnp.minimum(within, cut_first - 1),
    ])
    kept_inner = (1 - parity) * seg
    kept_outer = seg - kept_inner

    small = STEP // 2

    def add_whole(out, start, index, rows=BLK, step=STEP, first=0):
        targets = take_block(landed, start, 1)
        return add_rows(out, targets, places_w, [(arrived[index], 0)], rows, step, first)

    def add_cut(out, start, index, first):
        targets = take_block(landed, start + seg // 2, seg // 2)
        pieces = [(finished, first), (arrived[index], 0)]
        return add_rows(out, targets, places_c, pieces, cut, small, thin)

    at_i, arrived[5], out = after((at, arrived[5], base))
    whole_row(at_i, False, BLK, BLK, row_side, outer_row(BLK))
    out = add_rows(
        out, take_block(landed, kept_inner, seg // 2), places_q, [(arrived[k], 0) for k in range(4)], half
    )
    at_i, arrived[6], out = after((at, arrived[6], out))
    cut_rows(at_i, False, row_side, outer_row(local_rows - cut))
    at_i, arrived[7], out = after((at, arrived[7], out))
    whole_row(at_i, False, 2 * BLK, BLK, row_side, outer_row(2 * BLK))
    out = add_cut(out, kept_inner, 4, 0)
    out = add_whole(out, kept_inner + seg // 2, 5, thin, small)
    out = add_whole(out, kept_outer, 6)
    at_i, arrived[8], out = after((at, arrived[8], out))
    whole_row(at_i, False, 3 * BLK, STEP, row_side, outer_row(3 * BLK))
    out = add_whole(out, kept_outer + 1, 7)
    out = add_cut(out, kept_outer, 8, cut)
    at_i, arrived[9], out = after((at, arrived[9], out))
    whole_row(at_i, False, 3 * BLK + STEP, small, row_side, outer_row(3 * BLK + STEP))
    out = add_whole(out, kept_outer + 2, 9)
    out = add_whole(out, kept_outer + 3, 10, STEP)
    out = add_whole(out, kept_outer + 3, 11, small, small // 2, STEP)
    factor = jnp.concatenate([factor_a, factor_b], axis=0)
    return factor[None], out[None]


def solution(mesh):
    placed = (
        P("front", "row", "col"),
        P("front", ("row", "col"), None),
        P("front", None, None),
        P("front", None),
        P("front", None),
        P("front", "row", "col"),
    )
    return jax.shard_map(
        shards,
        mesh=mesh,
        in_specs=placed,
        out_specs=(P("front", ("row", "col"), None), P("front", "row", "col")),
        check_vma=False,
    )
```

```python
import functools

import jax
import jax.numpy as jnp
from jax import lax
from jax.experimental import pallas as pl
from jax.experimental.pallas import tpu as pltpu
from jax.sharding import PartitionSpec as P

BLK = 256
NT = (((1,), (1,)), ((), ()))
VMEM_LIMIT = 48 * 1024 * 1024
STEP = 128
MAP_ROWS = 16


def block_inverse(mapping):
    block_total = mapping.shape[0]
    target = jnp.arange(block_total, dtype=jnp.int32)
    matches = (mapping[:, None] == target[None, :]).astype(jnp.int32)
    return jnp.sum(matches * target[:, None], axis=0)


SMALL = pl.CostEstimate(flops=1, bytes_accessed=1, transcendentals=0)


def update_kernel(unit, col_unit, at_ref, front_ref, factor_ref, col_ref, out_ref):
    first = col_unit(pl.program_id(1)) * unit
    col = col_ref[pl.ds(pl.multiple_of(first, unit), unit), :]
    product = lax.dot_general(factor_ref[...], col, NT, preferred_element_type=jnp.float32)
    out_ref[...] = (front_ref[...].astype(jnp.float32) - product).astype(jnp.bfloat16)


def updated_rows(front, at, front_row, front_col, factor, factor_row, col_side, col_unit, grid, height, unit):
    pivots = factor.shape[1]
    return pl.pallas_call(
        functools.partial(update_kernel, unit, col_unit),
        grid_spec=pltpu.PrefetchScalarGridSpec(
            num_scalar_prefetch=1,
            grid=grid,
            in_specs=[
                pl.BlockSpec((height, unit), lambda i, j, at: (front_row(i, at), front_col(j, at))),
                pl.BlockSpec((height, pivots), lambda i, j, at: (factor_row(i, at), 0)),
                pl.BlockSpec(col_side.shape, lambda i, j, at: (0, 0)),
            ],
            out_specs=pl.BlockSpec((height, unit), lambda i, j, at: (i, j)),
        ),
        out_shape=jax.ShapeDtypeStruct((grid[0] * height, grid[1] * unit), jnp.bfloat16),
        compiler_params=pltpu.CompilerParams(vmem_limit_bytes=VMEM_LIMIT),
        cost_estimate=SMALL,
    )(at, front, factor, col_side)


def pick_kernel(at_ref, front_ref, out_ref):
    out_ref[...] = front_ref[...]


def picked_rows(front, at, first_row, rows, unit, stride, offset):
    units = front.shape[1] // unit // stride
    return pl.pallas_call(
        pick_kernel,
        grid_spec=pltpu.PrefetchScalarGridSpec(
            num_scalar_prefetch=1,
            grid=(units,),
            in_specs=[pl.BlockSpec(
                (pl.Element(rows), pl.Element(unit)),
                lambda j, at: (first_row(0, at), (j * stride + offset) * unit),
            )],
            out_specs=pl.BlockSpec((rows, unit), lambda j, at: (0, j)),
        ),
        out_shape=jax.ShapeDtypeStruct((rows, units * unit), jnp.bfloat16),
        compiler_params=pltpu.CompilerParams(vmem_limit_bytes=VMEM_LIMIT),
        cost_estimate=SMALL,
    )(at, front)


def assemble_kernel(plan, sources, at_ref, *refs):
    outs, sem = refs[sources:-1], refs[-1]
    for step, (out, first, rows, choice, options) in enumerate(plan):
        chosen = choice(at_ref)
        for value, (source, start) in options.items():
            @pl.when(chosen == value)
            def _():
                pltpu.make_async_copy(
                    refs[source].at[pl.ds(start, rows)], outs[out].at[pl.ds(first, rows)], sem.at[step]
                ).start()
    for step, (out, first, rows, _, options) in enumerate(plan):
        source, start = next(iter(options.values()))
        pltpu.make_async_copy(
            refs[source].at[pl.ds(start, rows)], outs[out].at[pl.ds(first, rows)], sem.at[step]
        ).wait()


def assembled(at, sources, plan, out_rows):
    width = sources[0].shape[1]
    return pl.pallas_call(
        functools.partial(assemble_kernel, plan, len(sources)),
        grid_spec=pltpu.PrefetchScalarGridSpec(
            num_scalar_prefetch=1,
            grid=(1,),
            in_specs=[pl.BlockSpec(memory_space=pl.ANY)] * len(sources),
            out_specs=[pl.BlockSpec((rows, width), lambda i, at: (0, 0)) for rows in out_rows],
            scratch_shapes=[pltpu.SemaphoreType.DMA((len(plan),))],
        ),
        out_shape=[jax.ShapeDtypeStruct((rows, width), jnp.bfloat16) for rows in out_rows],
        compiler_params=pltpu.CompilerParams(vmem_limit_bytes=VMEM_LIMIT),
        cost_estimate=SMALL,
    )(at, *sources)


def base_kernel(blocks, target_ref, own_ref, place_ref, front_ref, factor_ref, col_ref, given_ref, out_ref):
    factor = factor_ref[...]
    for block in range(blocks):
        here = pl.ds(block * BLK, BLK)
        own = pl.ds(pl.multiple_of(place_ref[block] * BLK, BLK), BLK)
        product = lax.dot_general(factor, col_ref[own, :], NT, preferred_element_type=jnp.float32)
        kept = (front_ref[:, own].astype(jnp.float32) - product).astype(jnp.bfloat16)
        out_ref[:, here] = given_ref[:, here].astype(jnp.float32) + kept.astype(jnp.float32)


def kept_rows(targets, owns, places, front, factor, col_side, given):
    count = targets.shape[0]
    cols = front.shape[1]
    pivots = factor.shape[1]
    return pl.pallas_call(
        functools.partial(base_kernel, cols // BLK),
        grid_spec=pltpu.PrefetchScalarGridSpec(
            num_scalar_prefetch=3,
            grid=(count,),
            in_specs=[
                pl.BlockSpec((BLK, cols), lambda i, targets, owns, places: (owns[i], 0)),
                pl.BlockSpec((BLK, pivots), lambda i, targets, owns, places: (owns[i], 0)),
                pl.BlockSpec(col_side.shape, lambda i, targets, owns, places: (0, 0)),
                pl.BlockSpec((BLK, cols), lambda i, targets, owns, places: (targets[i], 0)),
            ],
            out_specs=pl.BlockSpec((BLK, cols), lambda i, targets, owns, places: (targets[i], 0)),
        ),
        out_shape=jax.ShapeDtypeStruct(given.shape, jnp.float32),
        compiler_params=pltpu.CompilerParams(vmem_limit_bytes=VMEM_LIMIT),
        cost_estimate=SMALL,
    )(targets, owns, places, front, factor, col_side, given)


def add_kernel(blocks, pieces, target_ref, place_ref, *refs):
    base_ref, out_ref = refs[-2], refs[-1]
    for block in range(blocks):
        here = pl.ds(block * BLK, BLK)
        arrived = None
        for k in range(pieces):
            part = refs[k][:, pl.ds(pl.multiple_of(place_ref[1 + k, block] * BLK, BLK), BLK)]
            arrived = part if arrived is None else jnp.where(place_ref[0, block] == k, part, arrived)
        out_ref[:, here] = base_ref[:, here] + arrived.astype(jnp.float32)


def add_rows(base, targets, places, pieces, count, step=STEP, first=0):
    parts = BLK // step
    skip = first // step
    cols = base.shape[1]
    row = pl.BlockSpec(
        (step, cols),
        lambda i, targets, places: (targets[(i + skip) // parts] * parts + (i + skip) % parts, 0),
    )
    in_specs = [
        pl.BlockSpec((step, piece.shape[1]), functools.partial(lambda begin, i, *_: (i + begin, 0), begin // step))
        for piece, begin in pieces
    ]
    return pl.pallas_call(
        functools.partial(add_kernel, cols // BLK, len(pieces)),
        grid_spec=pltpu.PrefetchScalarGridSpec(
            num_scalar_prefetch=2, grid=(count // step,), in_specs=in_specs + [row], out_specs=row
        ),
        out_shape=jax.ShapeDtypeStruct(base.shape, jnp.float32),
        input_output_aliases={2 + len(pieces): 0},
        compiler_params=pltpu.CompilerParams(vmem_limit_bytes=VMEM_LIMIT),
        cost_estimate=SMALL,
    )(targets, places, *(piece for piece, _ in pieces), base)


def add_ahead_kernel(blocks, steps, target_ref, place_ref, piece_ref, base_ref, out_ref, held_ref):
    held_ref[...] = base_ref[...]
    out_ref[...] = base_ref[...]

    @pl.when(pl.program_id(0) < steps)
    def _():
        for block in range(blocks):
            here = pl.ds(block * BLK, BLK)
            arrived = piece_ref[:, pl.ds(pl.multiple_of(place_ref[1, block] * BLK, BLK), BLK)]
            out_ref[:, here] = base_ref[:, here] + arrived.astype(jnp.float32)


def add_ahead(base, targets, places, piece, step, first):
    parts = BLK // step
    steps = piece.shape[0] // step
    cols = base.shape[1]
    row = pl.BlockSpec((step, cols), lambda i, targets, places: (
        jnp.where(i < steps, targets[0] * parts + i, targets[1] * parts + first // step), 0
    ))
    return pl.pallas_call(
        functools.partial(add_ahead_kernel, cols // BLK, steps),
        grid_spec=pltpu.PrefetchScalarGridSpec(
            num_scalar_prefetch=2,
            grid=(steps + 1,),
            in_specs=[pl.BlockSpec((step, cols), lambda i, *_: (jnp.minimum(i, steps - 1), 0)), row],
            out_specs=[row, pl.BlockSpec((step, cols), lambda i, *_: (0, 0))],
        ),
        out_shape=[
            jax.ShapeDtypeStruct(base.shape, jnp.float32), jax.ShapeDtypeStruct((step, cols), jnp.float32)
        ],
        input_output_aliases={3: 0},
        compiler_params=pltpu.CompilerParams(vmem_limit_bytes=VMEM_LIMIT),
        cost_estimate=SMALL,
    )(targets, places, piece, base)


def add_held_kernel(blocks, target_ref, place_ref, piece_ref, held_ref, base_ref, out_ref):
    for block in range(blocks):
        here = pl.ds(block * BLK, BLK)
        arrived = piece_ref[:, pl.ds(pl.multiple_of(place_ref[1, block] * BLK, BLK), BLK)]
        out_ref[:, here] = held_ref[:, here] + arrived.astype(jnp.float32)


def add_held(base, target, places, piece, held, first):
    rows, cols = piece.shape
    step = rows // 2
    parts = BLK // step
    skip = first // step
    part = pl.BlockSpec((step, cols), lambda i, *_: (i, 0))
    return pl.pallas_call(
        functools.partial(add_held_kernel, cols // BLK),
        grid_spec=pltpu.PrefetchScalarGridSpec(
            num_scalar_prefetch=2,
            grid=(2,),
            in_specs=[part, part, pl.BlockSpec(memory_space=pl.ANY)],
            out_specs=pl.BlockSpec((step, cols), lambda i, target, places: (target[0] * parts + skip + i, 0)),
        ),
        out_shape=jax.ShapeDtypeStruct(base.shape, jnp.float32),
        input_output_aliases={4: 0},
        compiler_params=pltpu.CompilerParams(vmem_limit_bytes=VMEM_LIMIT),
        cost_estimate=SMALL,
    )(target, places, piece, held, base)


def take_block(table, first, count):
    return lax.dynamic_slice_in_dim(table, first, count, 0)


def hop(up_block, down_block, up, down):
    return lax.ppermute(up_block, "col", up), lax.ppermute(down_block, "col", down)


UP = [(0, 1), (1, 2), (2, 3)]
DOWN = [(1, 0), (2, 1), (3, 2)]
FAR = [(2, 3), (1, 0)]


def other_core(block):
    return lax.ppermute(block, "row", [(0, 1), (1, 0)])


def segment_at(segment, at_ref):
    away = segment - at_ref[0]
    far = jnp.where(away == 2, 4, 5)
    near = jnp.where(away == -1, 1, jnp.where(away == 1, 2, jnp.where(away == -2, 3, far)))
    return jnp.where(away == 0, 0, near)


def settled(array, table, turns):
    array, table = lax.optimization_barrier((array, table))
    for _ in range(turns):
        table = other_core(table)
    return array, table


def near_source(at_ref):
    own = segment_at(col_segment(False)(at_ref), at_ref)
    other = jnp.where((at_ref[0] == 1) | (at_ref[0] == 2), 3, 4)
    return jnp.where(not_owner(at_ref) == 0, own, other)


def options(sources, rows=0):
    return {k: (k, rows) for k in range(sources)}


def col_segment(far):
    def segment(at_ref):
        low = at_ref[0] % 2 * 2
        near = at_ref[0] // 2
        return low + (1 - near if far else near)
    return segment


def inner_segment(at_ref):
    return jnp.where(at_ref[2] == 1, 1, 2)


def at_segment(segment):
    return lambda at_ref: segment_at(segment(at_ref), at_ref)


def not_owner(at_ref):
    return jnp.where(at_ref[1] == at_ref[0] // 2, 0, 1)


def factor_of(panel, inverse, fill, first_row):
    local_rows = panel.shape[0]
    positions = (first_row + jnp.arange(local_rows, dtype=jnp.int32)) // BLK
    blocks = jnp.arange(fill.shape[0], dtype=jnp.int32)
    row_fill = jnp.sum(
        (positions[:, None] == blocks[None, :]).astype(jnp.int32) * fill[None, :], axis=1
    )
    masked = panel * row_fill[:, None].astype(jnp.bfloat16)
    return jnp.dot(masked, jnp.triu(inverse), preferred_element_type=jnp.float32).astype(jnp.bfloat16)


def from_sibling(block):
    route = []
    for low in range(0, lax.axis_size("front"), 2):
        route += [(low, low + 1), (low + 1, low)]
    return lax.ppermute(block, "front", route)


def shards(front, panel, inverse, fill, block_map, parent_front):
    front, panel, given = front[0], panel[0], parent_front[0]
    col_count = lax.axis_size("col")
    row_count = lax.axis_size("row")
    core = lax.axis_index("row")
    place = lax.axis_index("col")
    parity = lax.axis_index("front") % 2
    local_rows = panel.shape[0]
    tile_rows, tile_cols = front.shape
    half_blocks = tile_rows // 2 // BLK
    col_blocks = tile_cols // BLK
    seg = local_rows // BLK
    row_base = core * (tile_rows // BLK)
    source = block_inverse(block_map[0])
    col_source = take_block(source, place * col_blocks, col_blocks) - place * col_blocks
    first_row = (core * col_count + place) * local_rows

    closed = half_blocks % col_blocks == 0
    line = (
        row_count == 2 and col_count == 4 and closed and tile_rows == 2 * tile_cols
        and local_rows == 6 * BLK and 2 * local_rows == tile_cols
    )
    if not line:
        sibling_map = from_sibling(block_map[0])
        factor = factor_of(panel, inverse[0], fill[0], first_row)
        all_rows = lax.all_gather(factor, ("row", "col"), axis=0, tiled=True)
        row_side = take_block(all_rows, core * tile_rows, tile_rows)
        col_side = take_block(all_rows, place * tile_cols, tile_cols)
        sent = take_block(source, row_base + (1 - parity) * half_blocks, half_blocks) - row_base
        owns = take_block(source, row_base + parity * half_blocks, half_blocks) - row_base
        targets = jnp.arange(half_blocks, dtype=jnp.int32)
        grid = (half_blocks, 1)
        arrived = from_sibling(updated_rows(
            front, sent, lambda i, at: at[i], lambda j, at: j, row_side, lambda i, at: at[i], col_side,
            lambda j: j, grid, BLK, tile_cols,
        ))
        sibling_cols = take_block(block_inverse(sibling_map), place * col_blocks, col_blocks)
        sibling_cols = sibling_cols - place * col_blocks
        base = kept_rows(targets, owns, col_source, front, row_side, col_side, given)
        places = jnp.stack([jnp.zeros_like(sibling_cols), sibling_cols])
        out = add_rows(base, targets, places, [(arrived, 0)], half_blocks * BLK)
        return factor[None], out[None]

    half = local_rows // 2
    cut = local_rows * 3 // 8
    thin = local_rows // 8
    wide = local_rows // 3
    at = jnp.stack([place, core, parity]).astype(jnp.int32)
    after = lax.optimization_barrier

    def sent_row(inner, height):
        def row(at):
            sent = 1 - at[2]
            return sent * (half_blocks * BLK // height) + (at[2] if inner else sent) * (local_rows // height)
        return row

    def raw_rows(inner, first, rows):
        start = sent_row(inner, thin)
        skip = (local_rows - cut + first) // thin
        return picked_rows(front, at, lambda i, at: (start(at) + skip) * thin, rows, wide, 3, 2)

    raw = [raw_rows(*piece) for piece in ((True, 0, cut - thin), (False, 0, cut), (True, cut - thin, thin))]
    panel, raw[0] = after((panel, raw[0]))
    factor_a = factor_of(panel[:half], inverse[0], fill[0], first_row)
    raw[0] = from_sibling(raw[0])
    below_a, above_a = hop(factor_a, factor_a, UP, DOWN)
    factor_b = factor_of(panel[half:], inverse[0], fill[0], first_row + half)
    raw[1] = from_sibling(raw[1])
    near_part = assembled(
        at, [factor_a, below_a, above_a], [(0, 0, half, at_segment(col_segment(False)), options(3))], [half]
    )[0]
    near_other = other_core(near_part)
    raw[0], own_map = settled(raw[0], block_map[0], 1)
    below_a, above_a, own_map = after((below_a, above_a, own_map))
    below2_a, above2_a = hop(below_a, above_a, UP[1:], DOWN[:2])
    width = raw[2].shape[1]
    map_rows = jnp.pad(block_map[0].astype(jnp.bfloat16), (0, width - block_map.shape[1]))
    map_rows = jnp.broadcast_to(map_rows[None], (MAP_ROWS, width))
    part = factor_b[half - cut:].reshape(-1, width)
    raw[2] = jnp.concatenate([raw[2], part, map_rows], axis=0)
    raw[2] = from_sibling(raw[2])
    raw[1], own_map = settled(raw[1], own_map, 1)
    at_a, own_map = after((at, own_map))
    sources_a = [factor_a, below_a, above_a, below2_a, above2_a]
    near_a = assembled(
        at, [near_part, near_other], [(0, 0, half, not_owner, {0: (0, 0), 1: (1, 0)})], [half]
    )[0]
    inner_a = assembled(at_a, sources_a, [(0, 0, half, at_segment(inner_segment), options(5))], [half])[0]

    arrived = []

    def contribution(at, inner, first, rows, factor, factor_first, col_side, unit, units, front_col, col_unit):
        height = thin if rows % thin == 0 else min(rows, BLK)
        start = sent_row(inner, height)
        piece = updated_rows(
            front, at, lambda i, at: start(at) + first // height + i, front_col, factor,
            lambda i, at: factor_first(at, height) + i, col_side, col_unit, (rows // height, units), height, unit,
        )
        return piece

    def quarter(at, col_side, far, second):
        def front_col(j, at):
            near = at[0] // 2
            return (1 - near if far else near) * 2 + second
        return contribution(
            at, True, 0, half, inner_a, lambda at, height: 0, col_side, half, 1, front_col, lambda j: 0
        )

    piece = quarter(at_a, near_a, False, 0)
    at_f, piece = after((at_a, piece))
    arrived.append(from_sibling(piece))
    far_part = assembled(
        at_f, sources_a, [(0, 0, half, at_segment(col_segment(True)), options(5))], [half]
    )[0]
    far_a = assembled(
        at, [far_part, other_core(far_part)], [(0, 0, half, not_owner, {0: (0, 0), 1: (1, 0)})], [half]
    )[0]

    raw[2], own_map = settled(raw[2], own_map, 1)
    later, far_a, own_map, own_other = after((factor_b, far_a, own_map, other_core(factor_b)))
    arrived.append(from_sibling(quarter(at, far_a, True, 0)))
    below_b, above_b = hop(later, later, UP, DOWN)
    cross = lax.ppermute(later, ("row", "col"), [(2, col_count + 1), (col_count + 1, 2)])
    arrived[0], own_map = settled(arrived[0], own_map, 2)
    below_b, above_b, cross, own_map = after((below_b, above_b, cross, own_map))
    near_b = assembled(at, [factor_b, below_b, above_b, cross, own_other], [
        (0, 0, half, near_source, options(5))
    ], [half])[0]
    below2_b, above2_b = hop(below_b, above_b, UP[1:], DOWN[:2])
    arrived.append(from_sibling(quarter(at, near_b, False, 1)))
    sources_b = [factor_b, below_b, above_b, below2_b, above2_b]
    second = options(5)
    inner_b, far_part = assembled(at, sources_b, [
        (0, 0, half, at_segment(inner_segment), second),
        (1, 0, half, at_segment(col_segment(True)), second),
    ], [half] * 2)
    arrived[1], own_map = settled(arrived[1], own_map, 3)
    far_part, own_map = after((far_part, own_map))
    far_b = assembled(
        at, [far_part, other_core(far_part)], [(0, 0, half, not_owner, {0: (0, 0), 1: (1, 0)})], [half]
    )[0]
    arrived.append(from_sibling(quarter(at, far_b, True, 1)))
    col_side = assembled(at, [near_a, far_a, near_b, far_b], [
        (0, (2 * segment + k) * half, half, functools.partial(
            lambda segment, at_ref: jnp.where(at_ref[0] // 2 == segment, 0, 1), segment
        ), {0: (2 * k, 0), 1: (2 * k + 1, 0)})
        for segment in range(2) for k in range(2)
    ], [tile_cols])[0]

    def whole_row(at, inner, first, rows, factor, factor_first):
        arrived.append(from_sibling(contribution(
            at, inner, first, rows, factor, factor_first, col_side, half, 4, lambda j, at: j, lambda j: j
        )))

    def cut_rows(at, inner, factor, factor_first):
        arrived.append(from_sibling(contribution(
            at, inner, local_rows - cut, cut, factor, factor_first, col_side, wide, 4,
            lambda j, at: j + j // 2, lambda j: j + j // 2,
        )))

    arrived[2], own_map = settled(arrived[2], own_map, 1)
    at_i, own_map = after((at, own_map))
    cut_rows(at_i, True, inner_b, lambda at, height: 1)
    arrived[3], turned = settled(arrived[3], inner_b[:576], 2)
    whole_row(at, True, half, thin, turned, lambda at, height: 0)

    last_hop = assembled(at, [below2_a, above2_a, below2_b, above2_b], [
        (0, k * half, half, lambda at_ref: jnp.where(at_ref[0] == 2, 0, 1), {0: (2 * k, 0), 1: (2 * k + 1, 0)})
        for k in range(2)
    ], [local_rows])[0]
    last_hop, arrived[1] = after((last_hop, arrived[1]))
    far = lax.ppermute(last_hop, "col", FAR)
    row_side = assembled(at, [*sources_a, *sources_b, far], [
        (0, (2 * segment + k) * half, half, functools.partial(segment_at, segment), {
            **{j: (j + 5 * k, 0) for j in range(5)}, 5: (10, k * half)
        })
        for segment in range(4) for k in range(2)
    ], [tile_rows])[0]

    def outer_row(first):
        return lambda at, height: sent_row(False, height)(at) + first // height

    at_i, arrived[4] = after((at, arrived[4]))
    whole_row(at_i, False, 0, BLK, row_side, outer_row(0))

    sibling_map = raw[2][-1, :block_map.shape[1]].astype(jnp.int32)
    part = raw[2][thin:-MAP_ROWS].reshape(cut, -1)
    raw[2] = raw[2][:thin]
    part_below, part_above = hop(part, part, UP, DOWN)
    part_below, part_above, arrived[3] = after((part_below, part_above, arrived[3]))
    part_below2, part_above2 = hop(part_below, part_above, UP[1:], DOWN[:2])
    part_far = lax.ppermute(jnp.where(place == 2, part_below2, part_above2), "col", FAR)
    parts_near = [part, part_below, part_above, part_below2, part_above2]
    part_cols = assembled(at, parts_near, [
        (k, 0, wide, functools.partial(lambda k, at_ref: segment_at(at_ref[0] % 2 * 2 + k, at_ref), k),
         options(5, cut - wide))
        for k in range(2)
    ], [wide] * 2)
    others = [other_core(piece) for piece in part_cols]
    sibling_col = assembled(at, [*part_cols, *others], [
        (0, k * wide, wide, not_owner, {0: (k, 0), 1: (2 + k, 0)}) for k in range(2)
    ], [2 * wide])[0]
    part_rows = assembled(at, [*parts_near, part_far], [
        (0, k * cut, cut, functools.partial(
            lambda k, at_ref: segment_at(jnp.where(at_ref[2] == 0, 1 - k, 2 + k), at_ref), k
        ), options(6))
        for k in range(2)
    ], [2 * cut])[0]
    finished = updated_rows(
        jnp.concatenate([raw[0], raw[2], raw[1]], axis=0), at, lambda i, at: i, lambda j, at: j, part_rows, lambda i, at: i, sibling_col,
        lambda j: j, (2 * cut // thin, 2), thin, wide,
    )

    kept_base = row_base + parity * half_blocks
    source = block_inverse(own_map)
    owns = take_block(source, kept_base, half_blocks) - row_base
    col_source = take_block(source, place * col_blocks, col_blocks) - place * col_blocks
    base = kept_rows(
        jnp.arange(half_blocks, dtype=jnp.int32), owns, col_source, front, row_side, col_side, given
    )
    sibling_cols = take_block(block_inverse(sibling_map), place * col_blocks, col_blocks)
    sibling_cols = sibling_cols - place * col_blocks
    landed = take_block(sibling_map, kept_base, half_blocks) - kept_base
    segment, within = sibling_cols // seg, sibling_cols % seg
    cut_blocks = wide // BLK
    cut_first = seg - cut_blocks
    is_far = jnp.where(segment == place // 2, 0, 1)
    quarter_at = within % (seg // 2)
    places_q = jnp.stack([within // (seg // 2) * 2 + is_far] + [quarter_at] * 4)
    places_w = jnp.stack([jnp.zeros_like(sibling_cols), sibling_cols])
    places_c = jnp.stack([
        jnp.where(within < cut_first, 1, 0),
        segment * cut_blocks + jnp.maximum(within - cut_first, 0),
        segment * cut_first + jnp.minimum(within, cut_first - 1),
    ])
    kept_inner = (1 - parity) * seg
    kept_outer = seg - kept_inner

    small = STEP // 2

    def add_whole(out, start, index, rows=BLK, step=STEP, first=0):
        targets = take_block(landed, start, 1)
        return add_rows(out, targets, places_w, [(arrived[index], 0)], rows, step, first)

    def add_cut(out, start, index, first):
        targets = take_block(landed, start + seg // 2, seg // 2)
        pieces = [(finished, first), (arrived[index], 0)]
        return add_rows(out, targets, places_c, pieces, cut, small, thin)

    at_i, arrived[5], out = after((at, arrived[5], base))
    whole_row(at_i, False, BLK, BLK, row_side, outer_row(BLK))
    out = add_rows(
        out, take_block(landed, kept_inner, seg // 2), places_q, [(arrived[k], 0) for k in range(4)], half
    )
    at_i, arrived[6], out = after((at, arrived[6], out))
    cut_rows(at_i, False, row_side, outer_row(local_rows - cut))
    at_i, arrived[7], out = after((at, arrived[7], out))
    whole_row(at_i, False, 2 * BLK, BLK, row_side, outer_row(2 * BLK))
    out = add_cut(out, kept_inner, 4, 0)
    out = add_whole(out, kept_inner + seg // 2, 5, thin, small)
    out = add_whole(out, kept_outer, 6)
    at_i, arrived[8], out = after((at, arrived[8], out))
    whole_row(at_i, False, 3 * BLK, STEP, row_side, outer_row(3 * BLK))
    out = add_whole(out, kept_outer + 1, 7)
    out = add_cut(out, kept_outer, 8, cut)
    at_i, arrived[9], out = after((at, arrived[9], out))
    whole_row(at_i, False, 3 * BLK + STEP, small, row_side, outer_row(3 * BLK + STEP))
    out, held = add_ahead(out, take_block(landed, kept_outer + 2, 2), places_w, arrived[9], small, STEP)
    out = add_whole(out, kept_outer + 3, 10, STEP)
    out = add_held(out, take_block(landed, kept_outer + 3, 1), places_w, arrived[11], held, STEP)
    factor = jnp.concatenate([factor_a, factor_b], axis=0)
    return factor[None], out[None]


def solution(mesh):
    placed = (
        P("front", "row", "col"),
        P("front", ("row", "col"), None),
        P("front", None, None),
        P("front", None),
        P("front", None),
        P("front", "row", "col"),
    )
    return jax.shard_map(
        shards,
        mesh=mesh,
        in_specs=placed,
        out_specs=(P("front", ("row", "col"), None), P("front", "row", "col")),
        check_vma=False,
    )
```

```python
import functools

import jax
import jax.numpy as jnp
from jax import lax
from jax.experimental import pallas as pl
from jax.experimental.pallas import tpu as pltpu
from jax.sharding import PartitionSpec as P

BLK = 256
NT = (((1,), (1,)), ((), ()))
VMEM_LIMIT = 48 * 1024 * 1024
STEP = 128
MAP_ROWS = 8


def block_inverse(mapping):
    block_total = mapping.shape[0]
    target = jnp.arange(block_total, dtype=jnp.int32)
    matches = (mapping[:, None] == target[None, :]).astype(jnp.int32)
    return jnp.sum(matches * target[:, None], axis=0)


SMALL = pl.CostEstimate(flops=1, bytes_accessed=1, transcendentals=0)


def update_kernel(unit, col_unit, at_ref, front_ref, factor_ref, col_ref, out_ref):
    first = col_unit(pl.program_id(1)) * unit
    col = col_ref[pl.ds(pl.multiple_of(first, unit), unit), :]
    product = lax.dot_general(factor_ref[...], col, NT, preferred_element_type=jnp.float32)
    out_ref[...] = (front_ref[...].astype(jnp.float32) - product).astype(jnp.bfloat16)


def updated_rows(front, at, front_row, front_col, factor, factor_row, col_side, col_unit, grid, height, unit):
    pivots = factor.shape[1]
    return pl.pallas_call(
        functools.partial(update_kernel, unit, col_unit),
        grid_spec=pltpu.PrefetchScalarGridSpec(
            num_scalar_prefetch=1,
            grid=grid,
            in_specs=[
                pl.BlockSpec((height, unit), lambda i, j, at: (front_row(i, at), front_col(j, at))),
                pl.BlockSpec((height, pivots), lambda i, j, at: (factor_row(i, at), 0)),
                pl.BlockSpec(col_side.shape, lambda i, j, at: (0, 0)),
            ],
            out_specs=pl.BlockSpec((height, unit), lambda i, j, at: (i, j)),
        ),
        out_shape=jax.ShapeDtypeStruct((grid[0] * height, grid[1] * unit), jnp.bfloat16),
        compiler_params=pltpu.CompilerParams(vmem_limit_bytes=VMEM_LIMIT),
        cost_estimate=SMALL,
    )(at, front, factor, col_side)


def pick_kernel(at_ref, front_ref, out_ref):
    out_ref[...] = front_ref[...]


def picked_rows(front, at, first_row, rows, unit, stride, offset):
    units = front.shape[1] // unit // stride
    return pl.pallas_call(
        pick_kernel,
        grid_spec=pltpu.PrefetchScalarGridSpec(
            num_scalar_prefetch=1,
            grid=(units,),
            in_specs=[pl.BlockSpec(
                (pl.Element(rows), pl.Element(unit)),
                lambda j, at: (first_row(0, at), (j * stride + offset) * unit),
            )],
            out_specs=pl.BlockSpec((rows, unit), lambda j, at: (0, j)),
        ),
        out_shape=jax.ShapeDtypeStruct((rows, units * unit), jnp.bfloat16),
        compiler_params=pltpu.CompilerParams(vmem_limit_bytes=VMEM_LIMIT),
        cost_estimate=SMALL,
    )(at, front)


def assemble_kernel(plan, sources, at_ref, *refs):
    outs, sem = refs[sources:-1], refs[-1]
    for step, (out, first, rows, choice, options) in enumerate(plan):
        chosen = choice(at_ref)
        for value, (source, start) in options.items():
            @pl.when(chosen == value)
            def _():
                pltpu.make_async_copy(
                    refs[source].at[pl.ds(start, rows)], outs[out].at[pl.ds(first, rows)], sem.at[step]
                ).start()
    for step, (out, first, rows, _, options) in enumerate(plan):
        source, start = next(iter(options.values()))
        pltpu.make_async_copy(
            refs[source].at[pl.ds(start, rows)], outs[out].at[pl.ds(first, rows)], sem.at[step]
        ).wait()


def assembled(at, sources, plan, out_rows):
    width = sources[0].shape[1]
    return pl.pallas_call(
        functools.partial(assemble_kernel, plan, len(sources)),
        grid_spec=pltpu.PrefetchScalarGridSpec(
            num_scalar_prefetch=1,
            grid=(1,),
            in_specs=[pl.BlockSpec(memory_space=pl.ANY)] * len(sources),
            out_specs=[pl.BlockSpec((rows, width), lambda i, at: (0, 0)) for rows in out_rows],
            scratch_shapes=[pltpu.SemaphoreType.DMA((len(plan),))],
        ),
        out_shape=[jax.ShapeDtypeStruct((rows, width), jnp.bfloat16) for rows in out_rows],
        compiler_params=pltpu.CompilerParams(vmem_limit_bytes=VMEM_LIMIT),
        cost_estimate=SMALL,
    )(at, *sources)


def base_kernel(blocks, target_ref, own_ref, place_ref, front_ref, factor_ref, col_ref, given_ref, out_ref):
    factor = factor_ref[...]
    for block in range(blocks):
        here = pl.ds(block * BLK, BLK)
        own = pl.ds(pl.multiple_of(place_ref[block] * BLK, BLK), BLK)
        product = lax.dot_general(factor, col_ref[own, :], NT, preferred_element_type=jnp.float32)
        kept = (front_ref[:, own].astype(jnp.float32) - product).astype(jnp.bfloat16)
        out_ref[:, here] = given_ref[:, here].astype(jnp.float32) + kept.astype(jnp.float32)


def kept_rows(targets, owns, places, front, factor, col_side, given):
    count = targets.shape[0]
    cols = front.shape[1]
    pivots = factor.shape[1]
    return pl.pallas_call(
        functools.partial(base_kernel, cols // BLK),
        grid_spec=pltpu.PrefetchScalarGridSpec(
            num_scalar_prefetch=3,
            grid=(count,),
            in_specs=[
                pl.BlockSpec((BLK, cols), lambda i, targets, owns, places: (owns[i], 0)),
                pl.BlockSpec((BLK, pivots), lambda i, targets, owns, places: (owns[i], 0)),
                pl.BlockSpec(col_side.shape, lambda i, targets, owns, places: (0, 0)),
                pl.BlockSpec((BLK, cols), lambda i, targets, owns, places: (targets[i], 0)),
            ],
            out_specs=pl.BlockSpec((BLK, cols), lambda i, targets, owns, places: (targets[i], 0)),
        ),
        out_shape=jax.ShapeDtypeStruct(given.shape, jnp.float32),
        compiler_params=pltpu.CompilerParams(vmem_limit_bytes=VMEM_LIMIT),
        cost_estimate=SMALL,
    )(targets, owns, places, front, factor, col_side, given)


def add_kernel(blocks, pieces, target_ref, place_ref, *refs):
    base_ref, out_ref = refs[-2], refs[-1]
    for block in range(blocks):
        here = pl.ds(block * BLK, BLK)
        arrived = None
        for k in range(pieces):
            part = refs[k][:, pl.ds(pl.multiple_of(place_ref[1 + k, block] * BLK, BLK), BLK)]
            arrived = part if arrived is None else jnp.where(place_ref[0, block] == k, part, arrived)
        out_ref[:, here] = base_ref[:, here] + arrived.astype(jnp.float32)


def add_rows(base, targets, places, pieces, count, step=STEP, first=0):
    parts = BLK // step
    skip = first // step
    cols = base.shape[1]
    row = pl.BlockSpec(
        (step, cols),
        lambda i, targets, places: (targets[(i + skip) // parts] * parts + (i + skip) % parts, 0),
    )
    in_specs = [
        pl.BlockSpec((step, piece.shape[1]), functools.partial(lambda begin, i, *_: (i + begin, 0), begin // step))
        for piece, begin in pieces
    ]
    return pl.pallas_call(
        functools.partial(add_kernel, cols // BLK, len(pieces)),
        grid_spec=pltpu.PrefetchScalarGridSpec(
            num_scalar_prefetch=2, grid=(count // step,), in_specs=in_specs + [row], out_specs=row
        ),
        out_shape=jax.ShapeDtypeStruct(base.shape, jnp.float32),
        input_output_aliases={2 + len(pieces): 0},
        compiler_params=pltpu.CompilerParams(vmem_limit_bytes=VMEM_LIMIT),
        cost_estimate=SMALL,
    )(targets, places, *(piece for piece, _ in pieces), base)


def add_ahead_kernel(blocks, steps, target_ref, place_ref, piece_ref, base_ref, out_ref, held_ref):
    held_ref[...] = base_ref[...]
    out_ref[...] = base_ref[...]

    @pl.when(pl.program_id(0) < steps)
    def _():
        for block in range(blocks):
            here = pl.ds(block * BLK, BLK)
            arrived = piece_ref[:, pl.ds(pl.multiple_of(place_ref[1, block] * BLK, BLK), BLK)]
            out_ref[:, here] = base_ref[:, here] + arrived.astype(jnp.float32)


def add_ahead(base, targets, places, piece, step, first):
    parts = BLK // step
    steps = piece.shape[0] // step
    cols = base.shape[1]
    row = pl.BlockSpec((step, cols), lambda i, targets, places: (
        jnp.where(i < steps, targets[0] * parts + i, targets[1] * parts + first // step), 0
    ))
    return pl.pallas_call(
        functools.partial(add_ahead_kernel, cols // BLK, steps),
        grid_spec=pltpu.PrefetchScalarGridSpec(
            num_scalar_prefetch=2,
            grid=(steps + 1,),
            in_specs=[pl.BlockSpec((step, cols), lambda i, *_: (jnp.minimum(i, steps - 1), 0)), row],
            out_specs=[row, pl.BlockSpec((step, cols), lambda i, *_: (0, 0))],
        ),
        out_shape=[
            jax.ShapeDtypeStruct(base.shape, jnp.float32), jax.ShapeDtypeStruct((step, cols), jnp.float32)
        ],
        input_output_aliases={3: 0},
        compiler_params=pltpu.CompilerParams(vmem_limit_bytes=VMEM_LIMIT),
        cost_estimate=SMALL,
    )(targets, places, piece, base)


def add_held_kernel(blocks, target_ref, place_ref, piece_ref, held_ref, base_ref, out_ref):
    for block in range(blocks):
        here = pl.ds(block * BLK, BLK)
        arrived = piece_ref[:, pl.ds(pl.multiple_of(place_ref[1, block] * BLK, BLK), BLK)]
        out_ref[:, here] = held_ref[:, here] + arrived.astype(jnp.float32)


def add_held(base, target, places, piece, held, first):
    rows, cols = piece.shape
    step = rows // 2
    parts = BLK // step
    skip = first // step
    part = pl.BlockSpec((step, cols), lambda i, *_: (i, 0))
    return pl.pallas_call(
        functools.partial(add_held_kernel, cols // BLK),
        grid_spec=pltpu.PrefetchScalarGridSpec(
            num_scalar_prefetch=2,
            grid=(2,),
            in_specs=[part, part, pl.BlockSpec(memory_space=pl.ANY)],
            out_specs=pl.BlockSpec((step, cols), lambda i, target, places: (target[0] * parts + skip + i, 0)),
        ),
        out_shape=jax.ShapeDtypeStruct(base.shape, jnp.float32),
        input_output_aliases={4: 0},
        compiler_params=pltpu.CompilerParams(vmem_limit_bytes=VMEM_LIMIT),
        cost_estimate=SMALL,
    )(target, places, piece, held, base)


def take_block(table, first, count):
    return lax.dynamic_slice_in_dim(table, first, count, 0)


def hop(up_block, down_block, up, down):
    return lax.ppermute(up_block, "col", up), lax.ppermute(down_block, "col", down)


UP = [(0, 1), (1, 2), (2, 3)]
DOWN = [(1, 0), (2, 1), (3, 2)]
FAR = [(2, 3), (1, 0)]


def other_core(block):
    return lax.ppermute(block, "row", [(0, 1), (1, 0)])


def segment_at(segment, at_ref):
    away = segment - at_ref[0]
    far = jnp.where(away == 2, 4, 5)
    near = jnp.where(away == -1, 1, jnp.where(away == 1, 2, jnp.where(away == -2, 3, far)))
    return jnp.where(away == 0, 0, near)


def settled(array, table, turns):
    array, table = lax.optimization_barrier((array, table))
    for _ in range(turns):
        table = other_core(table)
    return array, table


def near_source(at_ref):
    own = segment_at(col_segment(False)(at_ref), at_ref)
    other = jnp.where((at_ref[0] == 1) | (at_ref[0] == 2), 3, 4)
    return jnp.where(not_owner(at_ref) == 0, own, other)


def options(sources, rows=0):
    return {k: (k, rows) for k in range(sources)}


def col_segment(far):
    def segment(at_ref):
        low = at_ref[0] % 2 * 2
        near = at_ref[0] // 2
        return low + (1 - near if far else near)
    return segment


def inner_segment(at_ref):
    return jnp.where(at_ref[2] == 1, 1, 2)


def at_segment(segment):
    return lambda at_ref: segment_at(segment(at_ref), at_ref)


def not_owner(at_ref):
    return jnp.where(at_ref[1] == at_ref[0] // 2, 0, 1)


def factor_of(panel, inverse, fill, first_row):
    local_rows = panel.shape[0]
    positions = (first_row + jnp.arange(local_rows, dtype=jnp.int32)) // BLK
    blocks = jnp.arange(fill.shape[0], dtype=jnp.int32)
    row_fill = jnp.sum(
        (positions[:, None] == blocks[None, :]).astype(jnp.int32) * fill[None, :], axis=1
    )
    masked = panel * row_fill[:, None].astype(jnp.bfloat16)
    return jnp.dot(masked, jnp.triu(inverse), preferred_element_type=jnp.float32).astype(jnp.bfloat16)


def from_sibling(block):
    route = []
    for low in range(0, lax.axis_size("front"), 2):
        route += [(low, low + 1), (low + 1, low)]
    return lax.ppermute(block, "front", route)


def shards(front, panel, inverse, fill, block_map, parent_front):
    front, panel, given = front[0], panel[0], parent_front[0]
    col_count = lax.axis_size("col")
    row_count = lax.axis_size("row")
    core = lax.axis_index("row")
    place = lax.axis_index("col")
    parity = lax.axis_index("front") % 2
    local_rows = panel.shape[0]
    tile_rows, tile_cols = front.shape
    half_blocks = tile_rows // 2 // BLK
    col_blocks = tile_cols // BLK
    seg = local_rows // BLK
    row_base = core * (tile_rows // BLK)
    source = block_inverse(block_map[0])
    col_source = take_block(source, place * col_blocks, col_blocks) - place * col_blocks
    first_row = (core * col_count + place) * local_rows

    closed = half_blocks % col_blocks == 0
    line = (
        row_count == 2 and col_count == 4 and closed and tile_rows == 2 * tile_cols
        and local_rows == 6 * BLK and 2 * local_rows == tile_cols
    )
    if not line:
        sibling_map = from_sibling(block_map[0])
        factor = factor_of(panel, inverse[0], fill[0], first_row)
        all_rows = lax.all_gather(factor, ("row", "col"), axis=0, tiled=True)
        row_side = take_block(all_rows, core * tile_rows, tile_rows)
        col_side = take_block(all_rows, place * tile_cols, tile_cols)
        sent = take_block(source, row_base + (1 - parity) * half_blocks, half_blocks) - row_base
        owns = take_block(source, row_base + parity * half_blocks, half_blocks) - row_base
        targets = jnp.arange(half_blocks, dtype=jnp.int32)
        grid = (half_blocks, 1)
        arrived = from_sibling(updated_rows(
            front, sent, lambda i, at: at[i], lambda j, at: j, row_side, lambda i, at: at[i], col_side,
            lambda j: j, grid, BLK, tile_cols,
        ))
        sibling_cols = take_block(block_inverse(sibling_map), place * col_blocks, col_blocks)
        sibling_cols = sibling_cols - place * col_blocks
        base = kept_rows(targets, owns, col_source, front, row_side, col_side, given)
        places = jnp.stack([jnp.zeros_like(sibling_cols), sibling_cols])
        out = add_rows(base, targets, places, [(arrived, 0)], half_blocks * BLK)
        return factor[None], out[None]

    half = local_rows // 2
    cut = local_rows * 3 // 8
    thin = local_rows // 8
    wide = local_rows // 3
    at = jnp.stack([place, core, parity]).astype(jnp.int32)
    after = lax.optimization_barrier

    def sent_row(inner, height):
        def row(at):
            sent = 1 - at[2]
            return sent * (half_blocks * BLK // height) + (at[2] if inner else sent) * (local_rows // height)
        return row

    def raw_rows(inner, first, rows):
        start = sent_row(inner, thin)
        skip = (local_rows - cut + first) // thin
        return picked_rows(front, at, lambda i, at: (start(at) + skip) * thin, rows, wide, 3, 2)

    raw = [raw_rows(*piece) for piece in ((True, 0, cut - thin), (False, 0, cut), (True, cut - thin, thin))]
    panel, raw[0] = after((panel, raw[0]))
    factor_a = factor_of(panel[:half], inverse[0], fill[0], first_row)
    raw[0] = from_sibling(raw[0])
    below_a, above_a = hop(factor_a, factor_a, UP, DOWN)
    factor_b = factor_of(panel[half:], inverse[0], fill[0], first_row + half)
    raw[1] = from_sibling(raw[1])
    near_part = assembled(
        at, [factor_a, below_a, above_a], [(0, 0, half, at_segment(col_segment(False)), options(3))], [half]
    )[0]
    near_other = other_core(near_part)
    raw[0], own_map = settled(raw[0], block_map[0], 1)
    below_a, above_a, own_map = after((below_a, above_a, own_map))
    below2_a, above2_a = hop(below_a, above_a, UP[1:], DOWN[:2])
    width = raw[2].shape[1]
    map_rows = jnp.pad(block_map[0].astype(jnp.bfloat16), (0, width - block_map.shape[1]))
    map_rows = jnp.broadcast_to(map_rows[None], (MAP_ROWS, width))
    part = factor_b[half - cut:].reshape(-1, width)
    raw[2] = jnp.concatenate([raw[2], part, map_rows], axis=0)
    raw[2] = from_sibling(raw[2])
    raw[1], own_map = settled(raw[1], own_map, 1)
    at_a, own_map = after((at, own_map))
    sources_a = [factor_a, below_a, above_a, below2_a, above2_a]
    near_a = assembled(
        at, [near_part, near_other], [(0, 0, half, not_owner, {0: (0, 0), 1: (1, 0)})], [half]
    )[0]
    inner_a = assembled(at_a, sources_a, [(0, 0, half, at_segment(inner_segment), options(5))], [half])[0]

    arrived = []

    def contribution(at, inner, first, rows, factor, factor_first, col_side, unit, units, front_col, col_unit):
        height = thin if rows % thin == 0 else min(rows, BLK)
        start = sent_row(inner, height)
        piece = updated_rows(
            front, at, lambda i, at: start(at) + first // height + i, front_col, factor,
            lambda i, at: factor_first(at, height) + i, col_side, col_unit, (rows // height, units), height, unit,
        )
        return piece

    def quarter(at, col_side, far, second):
        def front_col(j, at):
            near = at[0] // 2
            return (1 - near if far else near) * 2 + second
        return contribution(
            at, True, 0, half, inner_a, lambda at, height: 0, col_side, half, 1, front_col, lambda j: 0
        )

    piece = quarter(at_a, near_a, False, 0)
    at_f, piece = after((at_a, piece))
    arrived.append(from_sibling(piece))
    far_part = assembled(
        at_f, sources_a, [(0, 0, half, at_segment(col_segment(True)), options(5))], [half]
    )[0]
    far_a = assembled(
        at, [far_part, other_core(far_part)], [(0, 0, half, not_owner, {0: (0, 0), 1: (1, 0)})], [half]
    )[0]

    raw[2], own_map = settled(raw[2], own_map, 1)
    later, far_a, own_map, own_other = after((factor_b, far_a, own_map, other_core(factor_b)))
    arrived.append(from_sibling(quarter(at, far_a, True, 0)))
    below_b, above_b = hop(later, later, UP, DOWN)
    cross = lax.ppermute(later, ("row", "col"), [(2, col_count + 1), (col_count + 1, 2)])
    arrived[0], own_map = settled(arrived[0], own_map, 2)
    below_b, above_b, cross, own_map = after((below_b, above_b, cross, own_map))
    near_b = assembled(at, [factor_b, below_b, above_b, cross, own_other], [
        (0, 0, half, near_source, options(5))
    ], [half])[0]
    below2_b, above2_b = hop(below_b, above_b, UP[1:], DOWN[:2])
    arrived.append(from_sibling(quarter(at, near_b, False, 1)))
    sources_b = [factor_b, below_b, above_b, below2_b, above2_b]
    second = options(5)
    inner_b, far_part = assembled(at, sources_b, [
        (0, 0, half, at_segment(inner_segment), second),
        (1, 0, half, at_segment(col_segment(True)), second),
    ], [half] * 2)
    arrived[1], own_map = settled(arrived[1], own_map, 3)
    far_part, own_map = after((far_part, own_map))
    far_b = assembled(
        at, [far_part, other_core(far_part)], [(0, 0, half, not_owner, {0: (0, 0), 1: (1, 0)})], [half]
    )[0]
    arrived.append(from_sibling(quarter(at, far_b, True, 1)))
    col_side = assembled(at, [near_a, far_a, near_b, far_b], [
        (0, (2 * segment + k) * half, half, functools.partial(
            lambda segment, at_ref: jnp.where(at_ref[0] // 2 == segment, 0, 1), segment
        ), {0: (2 * k, 0), 1: (2 * k + 1, 0)})
        for segment in range(2) for k in range(2)
    ], [tile_cols])[0]

    def whole_row(at, inner, first, rows, factor, factor_first):
        arrived.append(from_sibling(contribution(
            at, inner, first, rows, factor, factor_first, col_side, half, 4, lambda j, at: j, lambda j: j
        )))

    def cut_rows(at, inner, factor, factor_first):
        arrived.append(from_sibling(contribution(
            at, inner, local_rows - cut, cut, factor, factor_first, col_side, wide, 4,
            lambda j, at: j + j // 2, lambda j: j + j // 2,
        )))

    arrived[2], own_map = settled(arrived[2], own_map, 1)
    at_i, own_map = after((at, own_map))
    cut_rows(at_i, True, inner_b, lambda at, height: 1)
    arrived[3], turned = settled(arrived[3], inner_b[:576], 2)
    whole_row(at, True, half, thin, turned, lambda at, height: 0)

    last_hop = assembled(at, [below2_a, above2_a, below2_b, above2_b], [
        (0, k * half, half, lambda at_ref: jnp.where(at_ref[0] == 2, 0, 1), {0: (2 * k, 0), 1: (2 * k + 1, 0)})
        for k in range(2)
    ], [local_rows])[0]
    last_hop, arrived[1] = after((last_hop, arrived[1]))
    far = lax.ppermute(last_hop, "col", FAR)
    row_side = assembled(at, [*sources_a, *sources_b, far], [
        (0, (2 * segment + k) * half, half, functools.partial(segment_at, segment), {
            **{j: (j + 5 * k, 0) for j in range(5)}, 5: (10, k * half)
        })
        for segment in range(4) for k in range(2)
    ], [tile_rows])[0]

    def outer_row(first):
        return lambda at, height: sent_row(False, height)(at) + first // height

    at_i, arrived[4] = after((at, arrived[4]))
    whole_row(at_i, False, 0, BLK, row_side, outer_row(0))

    sibling_map = raw[2][-1, :block_map.shape[1]].astype(jnp.int32)
    part = raw[2][thin:-MAP_ROWS].reshape(cut, -1)
    raw[2] = raw[2][:thin]
    part_below, part_above = hop(part, part, UP, DOWN)
    part_below, part_above, arrived[3] = after((part_below, part_above, arrived[3]))
    part_below2, part_above2 = hop(part_below, part_above, UP[1:], DOWN[:2])
    part_far = lax.ppermute(jnp.where(place == 2, part_below2, part_above2), "col", FAR)
    parts_near = [part, part_below, part_above, part_below2, part_above2]
    part_cols = assembled(at, parts_near, [
        (k, 0, wide, functools.partial(lambda k, at_ref: segment_at(at_ref[0] % 2 * 2 + k, at_ref), k),
         options(5, cut - wide))
        for k in range(2)
    ], [wide] * 2)
    others = [other_core(piece) for piece in part_cols]
    sibling_col = assembled(at, [*part_cols, *others], [
        (0, k * wide, wide, not_owner, {0: (k, 0), 1: (2 + k, 0)}) for k in range(2)
    ], [2 * wide])[0]
    part_rows = assembled(at, [*parts_near, part_far], [
        (0, k * cut, cut, functools.partial(
            lambda k, at_ref: segment_at(jnp.where(at_ref[2] == 0, 1 - k, 2 + k), at_ref), k
        ), options(6))
        for k in range(2)
    ], [2 * cut])[0]
    finished = updated_rows(
        jnp.concatenate([raw[0], raw[2], raw[1]], axis=0), at, lambda i, at: i, lambda j, at: j, part_rows, lambda i, at: i, sibling_col,
        lambda j: j, (2 * cut // thin, 2), thin, wide,
    )

    kept_base = row_base + parity * half_blocks
    source = block_inverse(own_map)
    owns = take_block(source, kept_base, half_blocks) - row_base
    col_source = take_block(source, place * col_blocks, col_blocks) - place * col_blocks
    base = kept_rows(
        jnp.arange(half_blocks, dtype=jnp.int32), owns, col_source, front, row_side, col_side, given
    )
    sibling_cols = take_block(block_inverse(sibling_map), place * col_blocks, col_blocks)
    sibling_cols = sibling_cols - place * col_blocks
    landed = take_block(sibling_map, kept_base, half_blocks) - kept_base
    segment, within = sibling_cols // seg, sibling_cols % seg
    cut_blocks = wide // BLK
    cut_first = seg - cut_blocks
    is_far = jnp.where(segment == place // 2, 0, 1)
    quarter_at = within % (seg // 2)
    places_q = jnp.stack([within // (seg // 2) * 2 + is_far] + [quarter_at] * 4)
    places_w = jnp.stack([jnp.zeros_like(sibling_cols), sibling_cols])
    places_c = jnp.stack([
        jnp.where(within < cut_first, 1, 0),
        segment * cut_blocks + jnp.maximum(within - cut_first, 0),
        segment * cut_first + jnp.minimum(within, cut_first - 1),
    ])
    kept_inner = (1 - parity) * seg
    kept_outer = seg - kept_inner

    small = STEP // 2

    def add_whole(out, start, index, rows=BLK, step=STEP, first=0):
        targets = take_block(landed, start, 1)
        return add_rows(out, targets, places_w, [(arrived[index], 0)], rows, step, first)

    def add_cut(out, start, index, first):
        targets = take_block(landed, start + seg // 2, seg // 2)
        pieces = [(finished, first), (arrived[index], 0)]
        return add_rows(out, targets, places_c, pieces, cut, small, thin)

    at_i, arrived[5], out = after((at, arrived[5], base))
    whole_row(at_i, False, BLK, BLK, row_side, outer_row(BLK))
    out = add_rows(
        out, take_block(landed, kept_inner, seg // 2), places_q, [(arrived[k], 0) for k in range(4)], half
    )
    at_i, arrived[6], out = after((at, arrived[6], out))
    cut_rows(at_i, False, row_side, outer_row(local_rows - cut))
    at_i, arrived[7], out = after((at, arrived[7], out))
    whole_row(at_i, False, 2 * BLK, BLK, row_side, outer_row(2 * BLK))
    out = add_cut(out, kept_inner, 4, 0)
    out = add_whole(out, kept_inner + seg // 2, 5, thin, small)
    out = add_whole(out, kept_outer, 6)
    at_i, arrived[8], out = after((at, arrived[8], out))
    whole_row(at_i, False, 3 * BLK, STEP, row_side, outer_row(3 * BLK))
    out = add_whole(out, kept_outer + 1, 7)
    out = add_cut(out, kept_outer, 8, cut)
    at_i, arrived[9], out = after((at, arrived[9], out))
    whole_row(at_i, False, 3 * BLK + STEP, small, row_side, outer_row(3 * BLK + STEP))
    out, held = add_ahead(out, take_block(landed, kept_outer + 2, 2), places_w, arrived[9], small, STEP)
    out = add_whole(out, kept_outer + 3, 10, STEP)
    out = add_held(out, take_block(landed, kept_outer + 3, 1), places_w, arrived[11], held, STEP)
    factor = jnp.concatenate([factor_a, factor_b], axis=0)
    return factor[None], out[None]


def solution(mesh):
    placed = (
        P("front", "row", "col"),
        P("front", ("row", "col"), None),
        P("front", None, None),
        P("front", None),
        P("front", None),
        P("front", "row", "col"),
    )
    return jax.shard_map(
        shards,
        mesh=mesh,
        in_specs=placed,
        out_specs=(P("front", ("row", "col"), None), P("front", "row", "col")),
        check_vma=False,
    )
```
